512 devices in a mesh: heads: 8 (over z_lo, core), tokens: 64 (over x, y, z_hi).
Axes of the slice: x: 4, y: 8, z: 8 (z_hi: 2, z_lo: 4; z = z_hi * 4 + z_lo), core: 2. Of those that a mesh axis runs over, the one named last changes fastest.
Arguments:
- queries: bfloat16 [2, 8192, 2048], P(None, 'tokens', 'heads'), may hold values from -8.5 to 8.5, as said below
- keys: bfloat16 [2, 8192, 2048], P(None, 'tokens', 'heads'), may hold values from -6 to 6
- values: bfloat16 [2, 8192, 2048], P(None, 'tokens', 'heads'), may hold values from -6 to 6
- rates: float32 [2, 8, 8192], P(None, 'heads', 'tokens'), may hold values from 0.05 to 1
- fast_init: bfloat16 [8, 3, 256, 256], P('heads'), may hold values from -0.375 to 0.375
- out_gain: float32 [2048], P('heads'), may hold values from 0.25 to 1.75
Outputs:
- mixed: bfloat16 [2, 8192, 2048], P(None, 'tokens', 'heads')
- final_weights: bfloat16 [8, 3, 256, 256], P('heads')
The draws below stay inside these ranges and needn't reach their ends.
Inputs may be any that keep to these rules, and one draw needn't show every extreme that they name: queries are real-valued and of order one.
All inputs are finite; a program needn't handle non-finite values.
Results may differ from the reference program's by a relative error of at most 0.0095.
Values may be sent and summed in bfloat16 or wider, within the bound.
No kernel may reach another device: no remote copies, remote signals or barrier semaphores. Data moves between devices by JAX's collectives and lax.ppermute only.
A program may use at most 64 MiB of HBM per device.

```python
import math
import jax
import jax.numpy as jnp
from jax import lax

HEADS = 8
DH = 256
D = 2048
GROUPS = 2
NS_STEPS = 2
GROUP = 8192


def draw_queries(key, part):
    first = jax.random.fold_in(jax.random.fold_in(key, 11), 0)
    column_head = jnp.arange(D) // DH
    scale = 0.6 + 0.8 * column_head.astype(jnp.float32) / (HEADS - 1)
    base = jnp.clip(jax.random.normal(first, (GROUPS, GROUP, D), jnp.float32), -6.0, 6.0)
    return (base * scale[None, None, :]).astype(jnp.bfloat16)


def steps_of(own_key, dims, cuts, low, high):
    def one(position, shards_of):
        heights = jax.random.uniform(jax.random.fold_in(jax.random.fold_in(own_key, 6), position), (shards_of,), jnp.float32, low / len(cuts), high / len(cuts))
        return jnp.repeat(jnp.exp(heights), dims[position] // shards_of).reshape((-1,) + (1,) * (len(dims) - position - 1))

    loudness = one(*cuts[0])
    for cut in cuts[1:]:
        loudness = loudness * one(*cut)
    return loudness


def bell_draw(stream_key, extent, spread, bound, pieces=(), kind=jnp.bfloat16):
    drawn = spread * jax.random.normal(stream_key, extent, jnp.float32)
    if pieces:
        drawn = drawn * steps_of(stream_key, extent, pieces, -0.22, 0.18)
    return jnp.clip(drawn, -bound, bound).astype(kind)


def setup_inputs(seed: int = 0) -> dict:
    splits = jax.random.split(jax.random.key(seed), 7)
    return {
        "queries": draw_queries(jax.random.fold_in(splits[6], 71), 0),
        "keys": bell_draw(splits[1], (GROUPS, GROUP, D), 1.0, 6.0, ((1, 64), (2, 8))),
        "values": bell_draw(splits[2], (GROUPS, GROUP, D), 1.0, 6.0, ((1, 64), (2, 8))),
        "rates": jnp.clip(jnp.exp(math.log(1.0) - 2.9957323 * jax.random.uniform(splits[3], (GROUPS, HEADS, GROUP), jnp.float32) ** steps_of(splits[3], (GROUPS, HEADS, GROUP), ((1, 8), (2, 64)), -0.2, 0.2)), 0.05, 1.0),
        "fast_init": bell_draw(splits[4], (HEADS, 3, DH, DH), DH ** -0.5, 0.375, ((0, 8),)),
        "out_gain": jnp.clip(1.0 + 0.15 * jax.random.normal(splits[5], (D,), jnp.float32), 0.25, 1.75),
    }


coef_a = 3.4445
coef_b = -4.775
coef_c = 2.0315
step_size = 0.5

def newton(grads):
    squares = lax.optimization_barrier(jnp.sum(grads * grads, axis=(1, 2)))
    current = (grads / (jnp.sqrt(squares)[:, None, None] + 1e-07)).astype(jnp.bfloat16)
    for step in range(NS_STEPS):
        wide = current.astype(jnp.float32)
        gram = jnp.einsum('mij,mkj->mik', wide, wide).astype(jnp.bfloat16)
        gram_wide = gram.astype(jnp.float32)
        square = jnp.einsum('mij,mjk->mik', gram_wide, gram_wide)
        mixer = (coef_b * gram_wide + coef_c * square).astype(jnp.bfloat16)
        current = (coef_a * wide + jnp.einsum('mij,mjk->mik', mixer.astype(jnp.float32), wide)).astype(jnp.bfloat16)
    return current

def head_step(items):
    query, key_rows, value_rows, rate, weight = items
    gate_q = jnp.dot(query, weight[0], preferred_element_type=jnp.float32)
    up_q = jnp.dot(query, weight[1], preferred_element_type=jnp.float32)
    hidden_q = (jax.nn.silu(gate_q) * up_q).astype(jnp.bfloat16)
    output = jnp.dot(hidden_q, weight[2], preferred_element_type=jnp.float32)
    gate_k = jnp.dot(key_rows, weight[0], preferred_element_type=jnp.float32)
    up_k = jnp.dot(key_rows, weight[1], preferred_element_type=jnp.float32)
    sig = jax.nn.sigmoid(gate_k)
    hidden = (gate_k * sig * up_k).astype(jnp.bfloat16)
    scaled = (rate[:, None] * value_rows.astype(jnp.float32)).astype(jnp.bfloat16)
    back = jnp.dot(scaled, weight[2].T, preferred_element_type=jnp.float32)
    grad_gate = (back * up_k * sig * (1.0 + gate_k * (1.0 - sig))).astype(jnp.bfloat16)
    grad_up = (back * gate_k * sig).astype(jnp.bfloat16)
    g_gate = jnp.dot(key_rows.T, grad_gate, preferred_element_type=jnp.float32)
    g_up = jnp.dot(key_rows.T, grad_up, preferred_element_type=jnp.float32)
    g_down = jnp.dot(hidden.T, scaled, preferred_element_type=jnp.float32)
    update = newton(jnp.stack([g_gate, g_up, g_down], axis=0))
    fresh = (weight.astype(jnp.float32) + step_size * update.astype(jnp.float32)).astype(jnp.bfloat16)
    return (output, fresh)

def reference(queries, keys, values, rates, fast_init, out_gain):
    weights = fast_init
    mixed = []
    for block in range(GROUPS):
        query = queries[block].reshape(GROUP, HEADS, DH).transpose(1, 0, 2)
        key_rows = keys[block].reshape(GROUP, HEADS, DH).transpose(1, 0, 2)
        value_rows = values[block].reshape(GROUP, HEADS, DH).transpose(1, 0, 2)
        outputs, weights = lax.map(head_step, (query, key_rows, value_rows, rates[block], weights))
        joined = outputs.transpose(1, 0, 2).reshape(GROUP, D)
        meansq = lax.optimization_barrier(jnp.mean(joined * joined, axis=1, keepdims=True))
        mixed.append((joined / jnp.sqrt(meansq + 1e-06) * out_gain[None, :]).astype(jnp.bfloat16))
    return (jnp.stack(mixed, axis=0), weights)
```

```python
import jax
import jax.numpy as jnp
from jax import lax
from jax.experimental import pallas as pl
from jax.experimental.pallas import tpu as pltpu
from jax.sharding import PartitionSpec as P

D = 2048
DH = 256
NS_STEPS = 2
PEERS = 8
SHARE = 3 * DH // PEERS

coef_a = 3.4445
coef_b = -4.775
coef_c = 2.0315
step_size = 0.5

F32 = jnp.float32
BF16 = jnp.bfloat16


def token_index(x, y_hi, y_lo, z_hi):
    return ((x * 4 + y_hi) * 2 + y_lo) * 2 + z_hi


NEAR = [
    [token_index(x, y_hi, y_lo, z_hi) for x in range(4) for y_lo in range(2)]
    for y_hi in range(4)
    for z_hi in range(2)
]
FAR = [
    [token_index(x, y_hi, y_lo, z_hi) for y_hi in range(4) for z_hi in range(2)]
    for x in range(4)
    for y_lo in range(2)
]


def exchange(array, groups):
    return lax.all_to_all(array, "tokens", 0, 0, axis_index_groups=groups, tiled=True)


def mm(a, b, ca=1, cb=0):
    return lax.dot_general(a, b, (((ca,), (cb,)), ((), ())), preferred_element_type=F32)


def call(body, out_shape, *args, flops=0, scratch=()):
    outs = out_shape if isinstance(out_shape, (tuple, list)) else [out_shape]
    moved = sum(a.size * a.dtype.itemsize for a in (*args, *outs))
    return pl.pallas_call(
        body,
        out_shape=out_shape,
        in_specs=[pl.BlockSpec(memory_space=pltpu.VMEM)] * len(args),
        out_specs=jax.tree.map(lambda _: pl.BlockSpec(memory_space=pltpu.VMEM), out_shape),
        scratch_shapes=list(scratch),
        compiler_params=pltpu.CompilerParams(vmem_limit_bytes=30 * 2**20),
        cost_estimate=pl.CostEstimate(flops=flops, bytes_accessed=moved, transcendentals=0),
    )(*args)


def scale_rows(rate_row, rows):
    tall = jnp.transpose(jnp.broadcast_to(rate_row, (128, rate_row.shape[1])))
    return (jnp.concatenate([tall, tall], axis=1) * rows.astype(F32)).astype(BF16)


def back_terms(keys, scaled, gate_w, up_w, down_w):
    gate = mm(keys, gate_w)
    up = mm(keys, up_w)
    back = mm(scaled, down_w, 1, 1)
    sig = jax.nn.sigmoid(gate)
    hidden = (gate * sig * up).astype(BF16)
    grad_gate = (back * up * sig * (1.0 + gate * (1.0 - sig))).astype(BF16)
    grad_up = (back * gate * sig).astype(BF16)
    return hidden, grad_gate, grad_up


def put_grads(out_ref, which, grad):
    grad = grad.astype(BF16)
    done = 0
    while done < DH:
        row = which * DH + done
        peer, inside = row // SHARE, row % SHARE
        count = min(SHARE - inside, DH - done)
        out_ref[peer, pl.ds(inside, count)] = grad[done : done + count]
        done += count


def first_kernel(k_ref, v_ref, r_ref, w_ref, grads_ref, ahead_ref):
    keys = k_ref[0]
    scaled = scale_rows(r_ref[0], v_ref[0])
    hidden, grad_gate, grad_up = back_terms(keys, scaled, w_ref[0, 0], w_ref[0, 1], w_ref[0, 2])
    put_grads(grads_ref, 0, mm(keys, grad_gate, 0, 0))
    put_grads(grads_ref, 1, mm(keys, grad_up, 0, 0))
    put_grads(grads_ref, 2, mm(hidden, scaled, 0, 0))
    later_keys = k_ref[1]
    later_scaled = scale_rows(r_ref[1], v_ref[1])
    ahead_ref[0] = later_keys
    ahead_ref[1] = later_scaled


def share_kernel(parts_ref, copies_ref):
    total = parts_ref[0].astype(F32)
    for peer in range(1, PEERS):
        total = total + parts_ref[peer].astype(F32)
    total = total.astype(BF16)
    for peer in range(PEERS):
        copies_ref[peer] = total


def newton_update(grads_ref, w_ref):
    stacked = grads_ref[...].reshape(3, DH, DH)
    current = []
    for m in range(3):
        wide = stacked[m].astype(F32)
        square = jnp.sum(jnp.sum(wide * wide, axis=0, keepdims=True), axis=1, keepdims=True)
        current.append((wide / (jnp.sqrt(square) + 1e-07)).astype(BF16))
    for step in range(NS_STEPS):
        grams = [mm(x, x, 1, 1).astype(BF16) for x in current]
        squares = [mm(a, a) for a in grams]
        mixers = [
            (coef_b * a.astype(F32) + coef_c * s).astype(BF16) for a, s in zip(grams, squares)
        ]
        products = [mm(b, x) for b, x in zip(mixers, current)]
        current = [(coef_a * x.astype(F32) + p).astype(BF16) for x, p in zip(current, products)]
    return [
        (w_ref[0, m].astype(F32) + step_size * current[m].astype(F32)).astype(BF16)
        for m in range(3)
    ]


def middle_kernel(grads_ref, w_ref, ahead_ref, fresh_ref, out_ref, hid_ref, dg_ref, du_ref):
    fresh = newton_update(grads_ref, w_ref)
    for m in range(3):
        fresh_ref[0, m] = fresh[m]
    step = 2
    for start in range(0, PEERS, step):
        keys = ahead_ref[start : start + step, 0].reshape(step * 128, DH)
        scaled = ahead_ref[start : start + step, 1].reshape(step * 128, DH)
        hidden, grad_gate, grad_up = back_terms(
            keys, scaled, fresh_ref[0, 0], fresh_ref[0, 1], fresh_ref[0, 2]
        )
        rows = pl.ds(start * 128, step * 128)
        hid_ref[rows] = hidden
        dg_ref[rows] = grad_gate
        du_ref[rows] = grad_up
    all_keys = ahead_ref[:, 0].reshape(PEERS * 128, DH)
    all_scaled = ahead_ref[:, 1].reshape(PEERS * 128, DH)
    put_grads(out_ref, 0, mm(all_keys, dg_ref[...], 0, 0))
    put_grads(out_ref, 1, mm(all_keys, du_ref[...], 0, 0))
    put_grads(out_ref, 2, mm(hid_ref[...], all_scaled, 0, 0))


def last_kernel(grads_ref, w_ref, fresh_ref):
    fresh = newton_update(grads_ref, w_ref)
    for m in range(3):
        fresh_ref[0, m] = fresh[m]


def query_kernel(q_ref, w0_ref, w1_ref, y_ref, squares_ref):
    for block, w_ref in enumerate((w0_ref, w1_ref)):
        gate = mm(q_ref[block], w_ref[0, 0])
        up = mm(q_ref[block], w_ref[0, 1])
        hidden = (gate * jax.nn.sigmoid(gate) * up).astype(BF16)
        out = mm(hidden, w_ref[0, 2])
        y_ref[block] = out
        sums = jnp.sum(out * out, axis=1, keepdims=True)
        row = jnp.transpose(jnp.broadcast_to(sums, (128, 128)))
        for peer in range(PEERS):
            squares_ref[peer, pl.ds(block, 1)] = row[:1]


def finish_kernel(y_ref, squares_ref, gain_ref, out_ref):
    total = squares_ref[0]
    for peer in range(1, PEERS):
        total = total + squares_ref[peer]
    root = jnp.sqrt(total / D + 1e-06)
    for block in range(2):
        tall = jnp.transpose(jnp.broadcast_to(root[block : block + 1], (128, 128)))
        both = jnp.concatenate([tall, tall], axis=1)
        out_ref[block] = (y_ref[block] / both * gain_ref[...]).astype(BF16)


def shaped(shape, dtype=BF16):
    return jax.ShapeDtypeStruct(shape, dtype)


def per_device(queries, keys, values, rates, fast_init, out_gain):
    pieces = shaped((PEERS, SHARE, DH))
    weights = shaped((1, 3, DH, DH))
    grads, ahead = call(
        first_kernel,
        (pieces, shaped((2, 128, DH))),
        keys, values, rates, fast_init, flops=10**8,
    )
    parts = exchange(grads, NEAR)
    ahead = lax.all_gather(ahead, "tokens", axis=0, axis_index_groups=FAR)
    parts = exchange(call(share_kernel, pieces, parts), FAR)
    whole = exchange(call(share_kernel, pieces, parts), NEAR)
    wide = [pltpu.VMEM((PEERS * 128, DH), BF16)] * 3
    fresh, grads = call(
        middle_kernel, (weights, pieces), whole, fast_init, ahead, flops=14 * 10**8, scratch=wide
    )
    parts = exchange(grads, NEAR)
    y, squares = call(
        query_kernel,
        (shaped((2, 128, DH), F32), shaped((PEERS, 2, 128), F32)),
        queries, fast_init, fresh, flops=10**8,
    )
    squares = lax.all_to_all(squares, "heads", 0, 0, tiled=True)
    whole = exchange(call(share_kernel, pieces, parts), NEAR)
    mixed = call(finish_kernel, shaped((2, 128, DH)), y, squares, out_gain.reshape(1, DH))
    final = call(last_kernel, weights, whole, fresh, flops=6 * 10**8)
    return mixed, final


def solution(mesh):
    in_specs = (
        P(None, "tokens", "heads"),
        P(None, "tokens", "heads"),
        P(None, "tokens", "heads"),
        P(None, "heads", "tokens"),
        P("heads", None, None, None),
        P("heads"),
    )
    out_specs = (P(None, "tokens", "heads"), P("heads", None, None, None))
    return jax.shard_map(
        per_device, mesh=mesh, in_specs=in_specs, out_specs=out_specs, check_vma=False
    )
```

```python
import jax
import jax.numpy as jnp
from jax import lax
from jax.experimental import pallas as pl
from jax.experimental.pallas import tpu as pltpu
from jax.sharding import PartitionSpec as P

D = 2048
DH = 256
NS_STEPS = 2
PEERS = 8
SHARE = 3 * DH // PEERS

coef_a = 3.4445
coef_b = -4.775
coef_c = 2.0315
step_size = 0.5

F32 = jnp.float32
BF16 = jnp.bfloat16


def token_index(x, y_hi, y_lo, z_hi):
    return ((x * 4 + y_hi) * 2 + y_lo) * 2 + z_hi


NEAR = [
    [token_index(x, y_hi, y_lo, z_hi) for x in range(4) for y_lo in range(2)]
    for y_hi in range(4)
    for z_hi in range(2)
]
FAR = [
    [token_index(x, y_hi, y_lo, z_hi) for y_hi in range(4) for z_hi in range(2)]
    for x in range(4)
    for y_lo in range(2)
]


def exchange(array, groups):
    return lax.all_to_all(array, "tokens", 0, 0, axis_index_groups=groups, tiled=True)


def mm(a, b, ca=1, cb=0):
    return lax.dot_general(a, b, (((ca,), (cb,)), ((), ())), preferred_element_type=F32)


def call(body, out_shape, *args, flops=0, scratch=(), space=pltpu.VMEM, limit=30):
    outs = out_shape if isinstance(out_shape, (tuple, list)) else [out_shape]
    moved = sum(a.size * a.dtype.itemsize for a in (*args, *outs))
    return pl.pallas_call(
        body,
        out_shape=out_shape,
        in_specs=[pl.BlockSpec(memory_space=space)] * len(args),
        out_specs=jax.tree.map(lambda _: pl.BlockSpec(memory_space=pltpu.VMEM), out_shape),
        scratch_shapes=list(scratch),
        compiler_params=pltpu.CompilerParams(vmem_limit_bytes=limit * 2**20),
        cost_estimate=pl.CostEstimate(flops=flops, bytes_accessed=moved, transcendentals=0),
    )(*args)


def scale_rows(rate_row, rows):
    tall = jnp.transpose(jnp.broadcast_to(rate_row, (128, rate_row.shape[1])))
    return (jnp.concatenate([tall, tall], axis=1) * rows.astype(F32)).astype(BF16)


def back_terms(keys, scaled, gate_w, up_w, down_w):
    gate = mm(keys, gate_w)
    up = mm(keys, up_w)
    back = mm(scaled, down_w, 1, 1)
    sig = jax.nn.sigmoid(gate)
    hidden = (gate * sig * up).astype(BF16)
    grad_gate = (back * up * sig * (1.0 + gate * (1.0 - sig))).astype(BF16)
    grad_up = (back * gate * sig).astype(BF16)
    return hidden, grad_gate, grad_up


def put_grads(out_ref, which, grad):
    grad = grad.astype(BF16)
    done = 0
    while done < DH:
        row = which * DH + done
        peer, inside = row // SHARE, row % SHARE
        count = min(SHARE - inside, DH - done)
        out_ref[peer, pl.ds(inside, count)] = grad[done : done + count]
        done += count


def local_grads(keys, scaled, gate_w, up_w, down_w, grads_ref):
    hidden, grad_gate, grad_up = back_terms(keys, scaled, gate_w, up_w, down_w)
    put_grads(grads_ref, 0, mm(keys, grad_gate, 0, 0))
    put_grads(grads_ref, 1, mm(keys, grad_up, 0, 0))
    put_grads(grads_ref, 2, mm(hidden, scaled, 0, 0))


def first_kernel(k_hbm, v_hbm, r_hbm, w_hbm, grads_ref, k_ref, v_ref, r_ref, w_ref, sems):
    pairs = ((w_hbm, w_ref), (k_hbm.at[0], k_ref), (v_hbm.at[0], v_ref), (r_hbm.at[0], r_ref))
    copies = [pltpu.make_async_copy(a, b, sems.at[n]) for n, (a, b) in enumerate(pairs)]
    for copy in copies:
        copy.start()
    for copy in copies:
        copy.wait()
    scaled = scale_rows(r_ref[...], v_ref[...])
    local_grads(k_ref[...], scaled, w_ref[0, 0], w_ref[0, 1], w_ref[0, 2], grads_ref)


def share_kernel(parts_ref, copies_ref):
    total = parts_ref[0].astype(F32)
    for peer in range(1, PEERS):
        total = total + parts_ref[peer].astype(F32)
    total = total.astype(BF16)
    for peer in range(PEERS):
        copies_ref[peer] = total


def newton_update(grads_ref, w_ref):
    stacked = grads_ref[...].reshape(3, DH, DH)
    current = []
    for m in range(3):
        wide = stacked[m].astype(F32)
        square = jnp.sum(jnp.sum(wide * wide, axis=0, keepdims=True), axis=1, keepdims=True)
        current.append((wide / (jnp.sqrt(square) + 1e-07)).astype(BF16))
    for step in range(NS_STEPS):
        grams = [mm(x, x, 1, 1).astype(BF16) for x in current]
        squares = [mm(a, a) for a in grams]
        mixers = [
            (coef_b * a.astype(F32) + coef_c * s).astype(BF16) for a, s in zip(grams, squares)
        ]
        products = [mm(b, x) for b, x in zip(mixers, current)]
        current = [(coef_a * x.astype(F32) + p).astype(BF16) for x, p in zip(current, products)]
    return [
        (w_ref[0, m].astype(F32) + step_size * current[m].astype(F32)).astype(BF16)
        for m in range(3)
    ]


def middle_kernel(grads_ref, w_ref, k_ref, v_ref, r_ref, fresh_ref, out_ref):
    fresh = newton_update(grads_ref, w_ref)
    for m in range(3):
        fresh_ref[0, m] = fresh[m]
    scaled = scale_rows(r_ref[1], v_ref[1])
    local_grads(k_ref[1], scaled, fresh[0], fresh[1], fresh[2], out_ref)


def last_kernel(grads_ref, w_ref, fresh_ref):
    fresh = newton_update(grads_ref, w_ref)
    for m in range(3):
        fresh_ref[0, m] = fresh[m]


def query_kernel(q_ref, w0_ref, w1_ref, y_ref, squares_ref):
    for block, w_ref in enumerate((w0_ref, w1_ref)):
        gate = mm(q_ref[block], w_ref[0, 0])
        up = mm(q_ref[block], w_ref[0, 1])
        hidden = (gate * jax.nn.sigmoid(gate) * up).astype(BF16)
        out = mm(hidden, w_ref[0, 2])
        y_ref[block] = out
        sums = jnp.sum(out * out, axis=1, keepdims=True)
        squares_ref[pl.ds(block, 1)] = jnp.transpose(jnp.broadcast_to(sums, (128, 128)))[:1]


def finish_kernel(y_ref, squares_ref, gain_ref, out_ref):
    root = jnp.sqrt(squares_ref[...] / D + 1e-06)
    for block in range(2):
        tall = jnp.transpose(jnp.broadcast_to(root[block : block + 1], (128, 128)))
        both = jnp.concatenate([tall, tall], axis=1)
        out_ref[block] = (y_ref[block] / both * gain_ref[...]).astype(BF16)


def shaped(shape, dtype=BF16):
    return jax.ShapeDtypeStruct(shape, dtype)


def add_partner(squares, bit):
    pairs = [(h, h ^ bit) for h in range(8)]
    return squares + lax.ppermute(squares, "heads", pairs)


def reduced(grads, beside=lambda: None):
    pieces = shaped((PEERS, SHARE, DH))
    aside = beside()
    parts, aside = lax.optimization_barrier((exchange(grads, NEAR), aside))
    parts = exchange(call(share_kernel, pieces, parts), FAR)
    if aside is not None:
        parts, aside = lax.optimization_barrier((parts, (aside[0], add_partner(aside[1], 2))))
    whole = exchange(call(share_kernel, pieces, parts), NEAR)
    if aside is None:
        return whole
    return whole, aside[0], add_partner(aside[1], 4)


def per_device(queries, keys, values, rates, fast_init, out_gain):
    pieces = shaped((PEERS, SHARE, DH))
    weights = shaped((1, 3, DH, DH))
    inputs = [
        pltpu.VMEM((1, 3, DH, DH), BF16),
        pltpu.VMEM((128, DH), BF16),
        pltpu.VMEM((128, DH), BF16),
        pltpu.VMEM((1, 128), F32),
    ]
    grads = call(
        first_kernel, pieces, keys, values, rates, fast_init, flops=10**8,
        scratch=[*inputs[1:], inputs[0], pltpu.SemaphoreType.DMA((4,))], space=pl.ANY, limit=58,
    )
    whole = reduced(grads)
    fresh, grads = call(
        middle_kernel, (weights, pieces), whole, fast_init, keys, values, rates, flops=7 * 10**8
    )

    def outputs():
        y, squares = call(
            query_kernel,
            (shaped((2, 128, DH), F32), shaped((2, 128), F32)),
            queries, fast_init, fresh, flops=10**8,
        )
        return y, add_partner(squares, 1)

    whole, y, squares = reduced(grads, outputs)
    mixed = call(finish_kernel, shaped((2, 128, DH)), y, squares, out_gain.reshape(1, DH))
    final = call(last_kernel, weights, whole, fresh, flops=6 * 10**8)
    return mixed, final


def solution(mesh):
    in_specs = (
        P(None, "tokens", "heads"),
        P(None, "tokens", "heads"),
        P(None, "tokens", "heads"),
        P(None, "heads", "tokens"),
        P("heads", None, None, None),
        P("heads"),
    )
    out_specs = (P(None, "tokens", "heads"), P("heads", None, None, None))
    return jax.shard_map(
        per_device, mesh=mesh, in_specs=in_specs, out_specs=out_specs, check_vma=False
    )
```

```python
import jax
import jax.numpy as jnp
from jax import lax
from jax.experimental import pallas as pl
from jax.experimental.pallas import tpu as pltpu
from jax.sharding import PartitionSpec as P

D = 2048
DH = 256
NS_STEPS = 2
PEERS = 8
SHARE = 3 * DH // PEERS

coef_a = 3.4445
coef_b = -4.775
coef_c = 2.0315
step_size = 0.5

F32 = jnp.float32
BF16 = jnp.bfloat16


def token_index(x, y_hi, y_lo, z_hi):
    return ((x * 4 + y_hi) * 2 + y_lo) * 2 + z_hi


NEAR = [
    [token_index(x, y_hi, y_lo, z_hi) for x in range(4) for y_lo in range(2)]
    for y_hi in range(4)
    for z_hi in range(2)
]
FAR = [
    [token_index(x, y_hi, y_lo, z_hi) for y_hi in range(4) for z_hi in range(2)]
    for x in range(4)
    for y_lo in range(2)
]


def token_pairs(move):
    places = [(x, h, l, z) for x in range(4) for h in range(4) for l in range(2) for z in range(2)]
    return [(token_index(*p), token_index(*move(*p))) for p in places]


def from_across(array):
    return lax.ppermute(array, "tokens", token_pairs(lambda x, h, l, z: (x, h, l, 1 - z)))


def from_along(array, steps):
    pairs = token_pairs(lambda x, h, l, z: (x, (h + steps) % 4, l, z))
    return lax.ppermute(array, "tokens", pairs)


def exchange(array, groups):
    return lax.all_to_all(array, "tokens", 0, 0, axis_index_groups=groups, tiled=True)


def mm(a, b, ca=1, cb=0):
    return lax.dot_general(a, b, (((ca,), (cb,)), ((), ())), preferred_element_type=F32)


def call(body, out_shape, *args, flops=0, scratch=(), space=pltpu.VMEM, limit=30):
    outs = out_shape if isinstance(out_shape, (tuple, list)) else [out_shape]
    moved = sum(a.size * a.dtype.itemsize for a in (*args, *outs))
    return pl.pallas_call(
        body,
        out_shape=out_shape,
        in_specs=[pl.BlockSpec(memory_space=space)] * len(args),
        out_specs=jax.tree.map(lambda _: pl.BlockSpec(memory_space=pltpu.VMEM), out_shape),
        scratch_shapes=list(scratch),
        compiler_params=pltpu.CompilerParams(vmem_limit_bytes=limit * 2**20),
        cost_estimate=pl.CostEstimate(flops=flops, bytes_accessed=moved, transcendentals=0),
    )(*args)


def scale_rows(rate_row, rows):
    tall = jnp.transpose(jnp.broadcast_to(rate_row, (128, rate_row.shape[1])))
    return (jnp.concatenate([tall, tall], axis=1) * rows.astype(F32)).astype(BF16)


def back_terms(keys, scaled, gate_w, up_w, down_w):
    gate = mm(keys, gate_w)
    up = mm(keys, up_w)
    back = mm(scaled, down_w, 1, 1)
    sig = jax.nn.sigmoid(gate)
    hidden = (gate * sig * up).astype(BF16)
    grad_gate = (back * up * sig * (1.0 + gate * (1.0 - sig))).astype(BF16)
    grad_up = (back * gate * sig).astype(BF16)
    return hidden, grad_gate, grad_up


def put_grads(out_ref, which, grad):
    grad = grad.astype(BF16)
    done = 0
    while done < DH:
        row = which * DH + done
        peer, inside = row // SHARE, row % SHARE
        count = min(SHARE - inside, DH - done)
        out_ref[peer, pl.ds(inside, count)] = grad[done : done + count]
        done += count


def local_grads(keys, scaled, gate_w, up_w, down_w, grads_ref):
    hidden, grad_gate, grad_up = back_terms(keys, scaled, gate_w, up_w, down_w)
    put_grads(grads_ref, 0, mm(keys, grad_gate, 0, 0))
    put_grads(grads_ref, 1, mm(keys, grad_up, 0, 0))
    put_grads(grads_ref, 2, mm(hidden, scaled, 0, 0))


def first_kernel(k_hbm, v_hbm, r_hbm, w_hbm, grads_ref, ahead_ref, k_ref, v_ref, r_ref, w_ref, sems):
    pairs = ((w_hbm, w_ref), (k_hbm, k_ref), (v_hbm, v_ref), (r_hbm, r_ref))
    copies = [pltpu.make_async_copy(a, b, sems.at[n]) for n, (a, b) in enumerate(pairs)]
    for copy in copies:
        copy.start()
    for copy in copies:
        copy.wait()
    scaled = scale_rows(r_ref[0], v_ref[0])
    local_grads(k_ref[0], scaled, w_ref[0, 0], w_ref[0, 1], w_ref[0, 2], grads_ref)
    ahead_ref[0] = k_ref[1]
    ahead_ref[1] = scale_rows(r_ref[1], v_ref[1])


def share_kernel(parts_ref, copies_ref):
    total = parts_ref[0].astype(F32)
    for peer in range(1, PEERS):
        total = total + parts_ref[peer].astype(F32)
    total = total.astype(BF16)
    for peer in range(PEERS):
        copies_ref[peer] = total


def newton_update(grads_ref, w_ref):
    stacked = grads_ref[...].reshape(3, DH, DH)
    current = []
    for m in range(3):
        wide = stacked[m].astype(F32)
        square = jnp.sum(jnp.sum(wide * wide, axis=0, keepdims=True), axis=1, keepdims=True)
        current.append((wide / (jnp.sqrt(square) + 1e-07)).astype(BF16))
    for step in range(NS_STEPS):
        grams = [mm(x, x, 1, 1).astype(BF16) for x in current]
        squares = [mm(a, a) for a in grams]
        mixers = [
            (coef_b * a.astype(F32) + coef_c * s).astype(BF16) for a, s in zip(grams, squares)
        ]
        products = [mm(b, x) for b, x in zip(mixers, current)]
        current = [(coef_a * x.astype(F32) + p).astype(BF16) for x, p in zip(current, products)]
    return [
        (w_ref[0, m].astype(F32) + step_size * current[m].astype(F32)).astype(BF16)
        for m in range(3)
    ]


def middle_kernel(grads_ref, w_ref, *refs):
    tokens, (fresh_ref, out_ref, k_ref, s_ref, hid_ref, dg_ref, du_ref) = refs[:4], refs[4:]
    fresh = newton_update(grads_ref, w_ref)
    for m in range(3):
        fresh_ref[0, m] = fresh[m]
    for n, token_ref in enumerate(tokens):
        rows = pl.ds(n * 256, 256)
        keys = token_ref[:, 0].reshape(256, DH)
        scaled = token_ref[:, 1].reshape(256, DH)
        k_ref[rows] = keys
        s_ref[rows] = scaled
        hid_ref[rows], dg_ref[rows], du_ref[rows] = back_terms(
            keys, scaled, fresh_ref[0, 0], fresh_ref[0, 1], fresh_ref[0, 2]
        )
    put_grads(out_ref, 0, mm(k_ref[...], dg_ref[...], 0, 0))
    put_grads(out_ref, 1, mm(k_ref[...], du_ref[...], 0, 0))
    put_grads(out_ref, 2, mm(hid_ref[...], s_ref[...], 0, 0))


def last_kernel(grads_ref, w_ref, fresh_ref):
    fresh = newton_update(grads_ref, w_ref)
    for m in range(3):
        fresh_ref[0, m] = fresh[m]


def query_kernel(q_ref, w0_ref, w1_ref, y_ref, squares_ref):
    for block, w_ref in enumerate((w0_ref, w1_ref)):
        gate = mm(q_ref[block], w_ref[0, 0])
        up = mm(q_ref[block], w_ref[0, 1])
        hidden = (gate * jax.nn.sigmoid(gate) * up).astype(BF16)
        out = mm(hidden, w_ref[0, 2])
        y_ref[block] = out
        sums = jnp.sum(out * out, axis=1, keepdims=True)
        squares_ref[pl.ds(block, 1)] = jnp.transpose(jnp.broadcast_to(sums, (128, 128)))[:1]


def finish_kernel(y_ref, squares_ref, gain_ref, out_ref):
    root = jnp.sqrt(squares_ref[...] / D + 1e-06)
    for block in range(2):
        tall = jnp.transpose(jnp.broadcast_to(root[block : block + 1], (128, 128)))
        both = jnp.concatenate([tall, tall], axis=1)
        out_ref[block] = (y_ref[block] / both * gain_ref[...]).astype(BF16)


def shaped(shape, dtype=BF16):
    return jax.ShapeDtypeStruct(shape, dtype)


def add_partner(squares, bit):
    pairs = [(h, h ^ bit) for h in range(8)]
    return squares + lax.ppermute(squares, "heads", pairs)


def together(*values):
    return lax.optimization_barrier(values)


def per_device(queries, keys, values, rates, fast_init, out_gain):
    pieces = shaped((PEERS, SHARE, DH))
    weights = shaped((1, 3, DH, DH))
    copied = [(2, 128, DH), (2, 128, DH), (2, 1, 128), (1, 3, DH, DH)]
    own = [pltpu.VMEM(shape, F32 if shape[1] == 1 else BF16) for shape in copied]
    grads, ahead = call(
        first_kernel, (pieces, shaped((2, 128, DH))), keys, values, rates, fast_init, flops=10**8,
        scratch=[*own, pltpu.SemaphoreType.DMA((4,))], space=pl.ANY, limit=58,
    )
    parts, across = together(exchange(grads, NEAR), from_across(ahead))
    shares = call(share_kernel, pieces, parts)
    pair = jnp.stack([ahead, across])
    shares, pair = together(shares, pair)
    parts, *others = together(exchange(shares, FAR), from_along(pair, 1), from_along(pair, 3))
    others.append(from_along(pair, 2))
    whole = exchange(call(share_kernel, pieces, parts), NEAR)
    wide = [pltpu.VMEM((PEERS * 128, DH), BF16)] * 5
    fresh, grads = call(
        middle_kernel, (weights, pieces), whole, fast_init, pair, *others, flops=14 * 10**8,
        scratch=wide,
    )
    y, squares = call(
        query_kernel,
        (shaped((2, 128, DH), F32), shaped((2, 128), F32)),
        queries, fast_init, fresh, flops=10**8,
    )
    squares = add_partner(add_partner(squares, 1), 2)
    parts, y, squares = together(exchange(grads, NEAR), y, squares)
    whole = exchange(call(share_kernel, pieces, parts), NEAR)
    squares = add_partner(squares, 4)
    mixed = call(finish_kernel, shaped((2, 128, DH)), y, squares, out_gain.reshape(1, DH))
    final = call(last_kernel, weights, whole, fresh, flops=6 * 10**8)
    return mixed, final


def solution(mesh):
    in_specs = (
        P(None, "tokens", "heads"),
        P(None, "tokens", "heads"),
        P(None, "tokens", "heads"),
        P(None, "heads", "tokens"),
        P("heads", None, None, None),
        P("heads"),
    )
    out_specs = (P(None, "tokens", "heads"), P("heads", None, None, None))
    return jax.shard_map(
        per_device, mesh=mesh, in_specs=in_specs, out_specs=out_specs, check_vma=False
    )
```

```python
import jax
import jax.numpy as jnp
from jax import lax
from jax.experimental import pallas as pl
from jax.experimental.pallas import tpu as pltpu
from jax.sharding import PartitionSpec as P

D = 2048
DH = 256
NS_STEPS = 2
PEERS = 8
SHARE = 3 * DH // PEERS

coef_a = 3.4445
coef_b = -4.775
coef_c = 2.0315
step_size = 0.5

F32 = jnp.float32
BF16 = jnp.bfloat16


def token_index(x, y_hi, y_lo, z_hi):
    return ((x * 4 + y_hi) * 2 + y_lo) * 2 + z_hi


NEAR = [
    [token_index(x, y_hi, y_lo, z_hi) for x in range(4) for y_lo in range(2)]
    for y_hi in range(4)
    for z_hi in range(2)
]
FAR = [
    [token_index(x, y_hi, y_lo, z_hi) for y_hi in range(4) for z_hi in range(2)]
    for x in range(4)
    for y_lo in range(2)
]
ALONG = [
    [token_index(x, y_hi, y_lo, z_hi) for y_hi in range(4)]
    for x in range(4)
    for y_lo in range(2)
    for z_hi in range(2)
]


def token_pairs(move):
    places = [(x, h, l, z) for x in range(4) for h in range(4) for l in range(2) for z in range(2)]
    return [(token_index(*p), token_index(*move(*p))) for p in places]


def from_across(array):
    return lax.ppermute(array, "tokens", token_pairs(lambda x, h, l, z: (x, h, l, 1 - z)))


def exchange(array, groups):
    return lax.all_to_all(array, "tokens", 0, 0, axis_index_groups=groups, tiled=True)


def mm(a, b, ca=1, cb=0):
    return lax.dot_general(a, b, (((ca,), (cb,)), ((), ())), preferred_element_type=F32)


def call(body, out_shape, *args, flops=0, scratch=(), space=pltpu.VMEM, limit=30):
    outs = out_shape if isinstance(out_shape, (tuple, list)) else [out_shape]
    moved = sum(a.size * a.dtype.itemsize for a in (*args, *outs))
    return pl.pallas_call(
        body,
        out_shape=out_shape,
        in_specs=[pl.BlockSpec(memory_space=space)] * len(args),
        out_specs=jax.tree.map(lambda _: pl.BlockSpec(memory_space=pltpu.VMEM), out_shape),
        scratch_shapes=list(scratch),
        compiler_params=pltpu.CompilerParams(vmem_limit_bytes=limit * 2**20),
        cost_estimate=pl.CostEstimate(flops=flops, bytes_accessed=moved, transcendentals=0),
    )(*args)


def scale_rows(rate_row, rows):
    tall = jnp.transpose(jnp.broadcast_to(rate_row, (128, rate_row.shape[1])))
    return (jnp.concatenate([tall, tall], axis=1) * rows.astype(F32)).astype(BF16)


def back_terms(keys, scaled, gate_w, up_w, down_w):
    gate = mm(keys, gate_w)
    up = mm(keys, up_w)
    back = mm(scaled, down_w, 1, 1)
    sig = jax.nn.sigmoid(gate)
    hidden = (gate * sig * up).astype(BF16)
    grad_gate = (back * up * sig * (1.0 + gate * (1.0 - sig))).astype(BF16)
    grad_up = (back * gate * sig).astype(BF16)
    return hidden, grad_gate, grad_up


def put_grads(out_ref, which, grad):
    grad = grad.astype(BF16)
    done = 0
    while done < DH:
        row = which * DH + done
        peer, inside = row // SHARE, row % SHARE
        count = min(SHARE - inside, DH - done)
        out_ref[peer, pl.ds(inside, count)] = grad[done : done + count]
        done += count


def local_grads(keys, scaled, gate_w, up_w, down_w, grads_ref):
    hidden, grad_gate, grad_up = back_terms(keys, scaled, gate_w, up_w, down_w)
    put_grads(grads_ref, 0, mm(keys, grad_gate, 0, 0))
    put_grads(grads_ref, 1, mm(keys, grad_up, 0, 0))
    put_grads(grads_ref, 2, mm(hidden, scaled, 0, 0))


def first_kernel(k_hbm, v_hbm, r_hbm, w_hbm, grads_ref, ahead_ref, k_ref, v_ref, r_ref, w_ref, sems):
    pairs = ((w_hbm, w_ref), (k_hbm, k_ref), (v_hbm, v_ref), (r_hbm, r_ref))
    copies = [pltpu.make_async_copy(a, b, sems.at[n]) for n, (a, b) in enumerate(pairs)]
    for copy in copies:
        copy.start()
    for copy in copies:
        copy.wait()
    scaled = scale_rows(r_ref[0], v_ref[0])
    local_grads(k_ref[0], scaled, w_ref[0, 0], w_ref[0, 1], w_ref[0, 2], grads_ref)
    ahead_ref[0] = k_ref[1]
    ahead_ref[1] = scale_rows(r_ref[1], v_ref[1])


def share_kernel(parts_ref, copies_ref):
    total = parts_ref[0].astype(F32)
    for peer in range(1, parts_ref.shape[0]):
        total = total + parts_ref[peer].astype(F32)
    total = total.astype(BF16)
    for peer in range(copies_ref.shape[0]):
        copies_ref[peer] = total


def newton_update(grads_ref, w_ref):
    stacked = grads_ref[...].reshape(3, DH, DH)
    current = []
    for m in range(3):
        wide = stacked[m].astype(F32)
        square = jnp.sum(jnp.sum(wide * wide, axis=0, keepdims=True), axis=1, keepdims=True)
        current.append((wide / (jnp.sqrt(square) + 1e-07)).astype(BF16))
    for step in range(NS_STEPS):
        grams = [mm(x, x, 1, 1).astype(BF16) for x in current]
        squares = [mm(a, a) for a in grams]
        mixers = [
            (coef_b * a.astype(F32) + coef_c * s).astype(BF16) for a, s in zip(grams, squares)
        ]
        products = [mm(b, x) for b, x in zip(mixers, current)]
        current = [(coef_a * x.astype(F32) + p).astype(BF16) for x, p in zip(current, products)]
    return [
        (w_ref[0, m].astype(F32) + step_size * current[m].astype(F32)).astype(BF16)
        for m in range(3)
    ]


def middle_kernel(grads_ref, w_ref, own_ref, across_ref, fresh_ref, out_ref):
    fresh = newton_update(grads_ref, w_ref)
    for m in range(3):
        fresh_ref[0, m] = fresh[m]
    keys = jnp.concatenate([own_ref[0], across_ref[0]], axis=0)
    scaled = jnp.concatenate([own_ref[1], across_ref[1]], axis=0)
    local_grads(keys, scaled, fresh[0], fresh[1], fresh[2], out_ref)


def last_kernel(grads_ref, w_ref, fresh_ref):
    fresh = newton_update(grads_ref, w_ref)
    for m in range(3):
        fresh_ref[0, m] = fresh[m]


def query_kernel(q_ref, w0_ref, w1_ref, gain_ref, y_ref, squares_ref):
    for block, w_ref in enumerate((w0_ref, w1_ref)):
        gate = mm(q_ref[block], w_ref[0, 0])
        up = mm(q_ref[block], w_ref[0, 1])
        hidden = (gate * jax.nn.sigmoid(gate) * up).astype(BF16)
        out = mm(hidden, w_ref[0, 2])
        y_ref[block] = out * gain_ref[...]
        sums = jnp.sum(out * out, axis=1, keepdims=True)
        squares_ref[pl.ds(block, 1)] = jnp.transpose(jnp.broadcast_to(sums, (128, 128)))[:1]


def finish_kernel(y_ref, squares_ref, out_ref):
    root = jnp.sqrt(squares_ref[...] / D + 1e-06)
    for block in range(2):
        tall = jnp.transpose(jnp.broadcast_to(root[block : block + 1], (128, 128)))
        both = jnp.concatenate([tall, tall], axis=1)
        out_ref[block] = (y_ref[block] / both).astype(BF16)


def shaped(shape, dtype=BF16):
    return jax.ShapeDtypeStruct(shape, dtype)


def add_partner(squares, bit):
    pairs = [(h, h ^ bit) for h in range(8)]
    return squares + lax.ppermute(squares, "heads", pairs)


def together(*values):
    return lax.optimization_barrier(values)


def per_device(queries, keys, values, rates, fast_init, out_gain):
    pieces = shaped((PEERS, SHARE, DH))
    weights = shaped((1, 3, DH, DH))
    copied = [(2, 128, DH), (2, 128, DH), (2, 1, 128), (1, 3, DH, DH)]
    own = [pltpu.VMEM(shape, F32 if shape[1] == 1 else BF16) for shape in copied]
    grads, ahead = call(
        first_kernel, (pieces, shaped((2, 128, DH))), keys, values, rates, fast_init, flops=10**8,
        scratch=[*own, pltpu.SemaphoreType.DMA((4,))], space=pl.ANY, limit=58,
    )
    share = shaped((4, SHARE, DH))
    parts = exchange(grads, NEAR)
    shares, ahead = together(call(share_kernel, pieces, parts), ahead)
    parts, across = together(exchange(shares, FAR), from_across(ahead))
    whole = exchange(call(share_kernel, pieces, parts), NEAR)
    fresh, grads = call(
        middle_kernel, (weights, pieces), whole, fast_init, ahead, across, flops=9 * 10**8
    )
    y, squares = call(
        query_kernel,
        (shaped((2, 128, DH), F32), shaped((2, 128), F32)),
        queries, fast_init, fresh, out_gain.reshape(1, DH), flops=10**8,
    )
    squares = add_partner(add_partner(squares, 1), 2)
    parts, y, squares = together(exchange(grads, NEAR), y, squares)
    shares = call(share_kernel, share, parts)
    parts, y, squares = together(exchange(shares, ALONG), y, add_partner(squares, 4))
    whole = exchange(call(share_kernel, pieces, parts), NEAR)
    mixed = call(finish_kernel, shaped((2, 128, DH)), y, squares)
    final = call(last_kernel, weights, whole, fresh, flops=6 * 10**8)
    return mixed, final


def solution(mesh):
    in_specs = (
        P(None, "tokens", "heads"),
        P(None, "tokens", "heads"),
        P(None, "tokens", "heads"),
        P(None, "heads", "tokens"),
        P("heads", None, None, None),
        P("heads"),
    )
    out_specs = (P(None, "tokens", "heads"), P("heads", None, None, None))
    return jax.shard_map(
        per_device, mesh=mesh, in_specs=in_specs, out_specs=out_specs, check_vma=False
    )
```

```python
import jax
import jax.numpy as jnp
from jax import lax
from jax.experimental import pallas as pl
from jax.experimental.pallas import tpu as pltpu
from jax.sharding import PartitionSpec as P

D = 2048
DH = 256
NS_STEPS = 2
PEERS = 8
SHARE = 3 * DH // PEERS
UNITS = DH // PEERS

coef_a = 3.4445
coef_b = -4.775
coef_c = 2.0315
step_size = 0.5

F32 = jnp.float32
BF16 = jnp.bfloat16


def token_index(x, y_hi, y_lo, z_hi):
    return ((x * 4 + y_hi) * 2 + y_lo) * 2 + z_hi


NEAR = [
    [token_index(x, y_hi, y_lo, z_hi) for x in range(4) for y_lo in range(2)]
    for y_hi in range(4)
    for z_hi in range(2)
]
FAR = [
    [token_index(x, y_hi, y_lo, z_hi) for y_hi in range(4) for z_hi in range(2)]
    for x in range(4)
    for y_lo in range(2)
]

def token_pairs(move):
    places = [(x, h, l, z) for x in range(4) for h in range(4) for l in range(2) for z in range(2)]
    return [(token_index(*p), token_index(*move(*p))) for p in places]


def from_beside(array):
    return lax.ppermute(array, "tokens", token_pairs(lambda x, h, l, z: (x, h, 1 - l, z)))


def from_along(array, steps):
    pairs = token_pairs(lambda x, h, l, z: ((x + steps) % 4, h, l, z))
    return lax.ppermute(array, "tokens", pairs)


def exchange(array, groups):
    return lax.all_to_all(array, "tokens", 0, 0, axis_index_groups=groups, tiled=True)


def mm(a, b, ca=1, cb=0):
    return lax.dot_general(a, b, (((ca,), (cb,)), ((), ())), preferred_element_type=F32)


def call(body, out_shape, *args, flops=0, scratch=(), space=pltpu.VMEM, limit=30):
    outs = out_shape if isinstance(out_shape, (tuple, list)) else [out_shape]
    moved = sum(a.size * a.dtype.itemsize for a in (*args, *outs))
    return pl.pallas_call(
        body,
        out_shape=out_shape,
        in_specs=[
            pl.BlockSpec(memory_space=pltpu.SMEM if a.dtype == jnp.int32 else space) for a in args
        ],
        out_specs=jax.tree.map(lambda _: pl.BlockSpec(memory_space=pltpu.VMEM), out_shape),
        scratch_shapes=list(scratch),
        compiler_params=pltpu.CompilerParams(vmem_limit_bytes=limit * 2**20),
        cost_estimate=pl.CostEstimate(flops=flops, bytes_accessed=moved, transcendentals=0),
    )(*args)


def scale_rows(rate_row, rows):
    tall = jnp.transpose(jnp.broadcast_to(rate_row, (128, rate_row.shape[1])))
    return (jnp.concatenate([tall, tall], axis=1) * rows.astype(F32)).astype(BF16)


def elementwise(gate, up, back):
    sig = jax.nn.sigmoid(gate)
    hidden = (gate * sig * up).astype(BF16)
    grad_gate = (back * up * sig * (1.0 + gate * (1.0 - sig))).astype(BF16)
    grad_up = (back * gate * sig).astype(BF16)
    return hidden, grad_gate, grad_up


def put_grads(out_ref, which, grad):
    grad = grad.astype(BF16)
    done = 0
    while done < DH:
        row = which * DH + done
        peer, inside = row // SHARE, row % SHARE
        count = min(SHARE - inside, DH - done)
        out_ref[peer, pl.ds(inside, count)] = grad[done : done + count]
        done += count


def local_grads(keys, scaled, gate_w, up_w, down_w, grads_ref):
    gate, up, back = mm(keys, gate_w), mm(keys, up_w), mm(scaled, down_w, 1, 1)
    hidden, grad_gate, grad_up = elementwise(gate, up, back)
    put_grads(grads_ref, 0, mm(keys, grad_gate, 0, 0))
    put_grads(grads_ref, 1, mm(keys, grad_up, 0, 0))
    put_grads(grads_ref, 2, mm(hidden, scaled, 0, 0))


def first_kernel(k_hbm, v_hbm, r_hbm, w_hbm, grads_ref, ahead_ref, k_ref, v_ref, r_ref, w_ref, sems):
    pairs = ((w_hbm, w_ref), (k_hbm, k_ref), (v_hbm, v_ref), (r_hbm, r_ref))
    copies = [pltpu.make_async_copy(a, b, sems.at[n]) for n, (a, b) in enumerate(pairs)]
    for copy in copies:
        copy.start()
    for copy in copies:
        copy.wait()
    scaled = scale_rows(r_ref[0], v_ref[0])
    local_grads(k_ref[0], scaled, w_ref[0, 0], w_ref[0, 1], w_ref[0, 2], grads_ref)
    ahead_ref[0] = k_ref[1]
    ahead_ref[1] = scale_rows(r_ref[1], v_ref[1])


def share_kernel(parts_ref, copies_ref):
    total = parts_ref[0].astype(F32)
    for peer in range(1, parts_ref.shape[0]):
        total = total + parts_ref[peer].astype(F32)
    total = total.astype(BF16)
    for peer in range(copies_ref.shape[0]):
        copies_ref[peer] = total


def newton_update(stacked, w_ref):
    current = []
    for m in range(3):
        wide = stacked[m].astype(F32)
        square = jnp.sum(jnp.sum(wide * wide, axis=0, keepdims=True), axis=1, keepdims=True)
        current.append((wide / (jnp.sqrt(square) + 1e-07)).astype(BF16))
    for step in range(NS_STEPS):
        grams = [mm(x, x, 1, 1).astype(BF16) for x in current]
        squares = [mm(a, a) for a in grams]
        mixers = [
            (coef_b * a.astype(F32) + coef_c * s).astype(BF16) for a, s in zip(grams, squares)
        ]
        products = [mm(b, x) for b, x in zip(mixers, current)]
        current = [(coef_a * x.astype(F32) + p).astype(BF16) for x, p in zip(current, products)]
    return [
        (w_ref[0, m].astype(F32) + step_size * current[m].astype(F32)).astype(BF16)
        for m in range(3)
    ]


def middle_kernel(grads_ref, w_ref, place_ref, *refs):
    tokens, (fresh_ref, out_ref, gate_ref, up_ref) = refs[:4], refs[4:]
    fresh = newton_update(grads_ref[...].reshape(3, DH, DH), w_ref)
    for m in range(3):
        fresh_ref[0, m] = fresh[m]
    gate_ref[...] = jnp.transpose(fresh[0])
    up_ref[...] = jnp.transpose(fresh[1])
    units = pl.ds(pl.multiple_of(place_ref[0] * UNITS, UNITS), UNITS)
    gate_w, up_w, down_w = gate_ref[units], up_ref[units], fresh_ref[0, 2, units]
    sums = [jnp.zeros((UNITS, DH), F32)] * 3
    for token_ref in tokens:
        keys = token_ref[:, 0].reshape(256, DH)
        scaled = token_ref[:, 1].reshape(256, DH)
        gate = mm(gate_w, keys, 1, 1)
        up = mm(up_w, keys, 1, 1)
        back = mm(down_w, scaled, 1, 1)
        hidden, grad_gate, grad_up = elementwise(gate, up, back)
        terms = mm(grad_gate, keys), mm(grad_up, keys), mm(hidden, scaled)
        sums = [s + t for s, t in zip(sums, terms)]
    for m in range(3):
        part = sums[m].astype(BF16)
        for peer in range(PEERS):
            out_ref[peer, pl.ds(m * UNITS, UNITS)] = part


def last_kernel(grads_ref, w_ref, fresh_ref):
    rows = [grads_ref[:, m * UNITS : (m + 1) * UNITS].reshape(DH, DH) for m in range(3)]
    stacked = [jnp.transpose(rows[0]), jnp.transpose(rows[1]), rows[2]]
    fresh = newton_update(stacked, w_ref)
    for m in range(3):
        fresh_ref[0, m] = fresh[m]


def query_kernel(q_ref, w0_ref, w1_ref, gain_ref, y_ref, squares_ref):
    for block, w_ref in enumerate((w0_ref, w1_ref)):
        gate = mm(q_ref[block], w_ref[0, 0])
        up = mm(q_ref[block], w_ref[0, 1])
        hidden = (gate * jax.nn.sigmoid(gate) * up).astype(BF16)
        out = mm(hidden, w_ref[0, 2])
        y_ref[block] = out * gain_ref[...]
        sums = jnp.sum(out * out, axis=1, keepdims=True)
        squares_ref[pl.ds(block, 1)] = jnp.transpose(jnp.broadcast_to(sums, (128, 128)))[:1]


def finish_kernel(y_ref, squares_ref, out_ref):
    root = jnp.sqrt(squares_ref[...] / D + 1e-06)
    for block in range(2):
        tall = jnp.transpose(jnp.broadcast_to(root[block : block + 1], (128, 128)))
        both = jnp.concatenate([tall, tall], axis=1)
        out_ref[block] = (y_ref[block] / both).astype(BF16)


def shaped(shape, dtype=BF16):
    return jax.ShapeDtypeStruct(shape, dtype)


def add_partner(squares, bit):
    pairs = [(h, h ^ bit) for h in range(8)]
    return squares + lax.ppermute(squares, "heads", pairs)


def together(*values):
    return lax.optimization_barrier(values)


def per_device(queries, keys, values, rates, fast_init, out_gain):
    pieces = shaped((PEERS, SHARE, DH))
    weights = shaped((1, 3, DH, DH))
    copied = [(2, 128, DH), (2, 128, DH), (2, 1, 128), (1, 3, DH, DH)]
    own = [pltpu.VMEM(shape, F32 if shape[1] == 1 else BF16) for shape in copied]
    grads, ahead = call(
        first_kernel, (pieces, shaped((2, 128, DH))), keys, values, rates, fast_init, flops=10**8,
        scratch=[*own, pltpu.SemaphoreType.DMA((4,))], space=pl.ANY, limit=58,
    )
    parts, beside = together(exchange(grads, NEAR), from_beside(ahead))
    shares = call(share_kernel, pieces, parts)
    shares, pair = together(shares, jnp.stack([ahead, beside]))
    parts, *others = together(
        exchange(shares, FAR), *(from_along(pair, steps) for steps in (1, 3, 2))
    )
    whole = exchange(call(share_kernel, pieces, parts), NEAR)
    token = lax.axis_index("tokens")
    place = (token // 16 * 2 + token // 2 % 2).reshape(1)
    fresh, shares = call(
        middle_kernel, (weights, pieces), whole, fast_init, place, pair, *others, flops=9 * 10**8,
        scratch=[pltpu.VMEM((DH, DH), BF16)] * 2,
    )
    y, squares = call(
        query_kernel,
        (shaped((2, 128, DH), F32), shaped((2, 128), F32)),
        queries, fast_init, fresh, out_gain.reshape(1, DH), flops=10**8,
    )
    for bit in (1, 2, 4):
        squares = add_partner(squares, bit)
    parts, y, squares = together(exchange(shares, FAR), y, squares)
    whole = exchange(call(share_kernel, pieces, parts), NEAR)
    mixed = call(finish_kernel, shaped((2, 128, DH)), y, squares)
    final = call(last_kernel, weights, whole, fresh, flops=6 * 10**8)
    return mixed, final


def solution(mesh):
    in_specs = (
        P(None, "tokens", "heads"),
        P(None, "tokens", "heads"),
        P(None, "tokens", "heads"),
        P(None, "heads", "tokens"),
        P("heads", None, None, None),
        P("heads"),
    )
    out_specs = (P(None, "tokens", "heads"), P("heads", None, None, None))
    return jax.shard_map(
        per_device, mesh=mesh, in_specs=in_specs, out_specs=out_specs, check_vma=False
    )
```

```python
import jax
import jax.numpy as jnp
from jax import lax
from jax.experimental import pallas as pl
from jax.experimental.pallas import tpu as pltpu
from jax.sharding import PartitionSpec as P

D = 2048
DH = 256
NS_STEPS = 2
PEERS = 8
SHARE = 3 * DH // PEERS
UNITS = DH // PEERS

coef_a = 3.4445
coef_b = -4.775
coef_c = 2.0315
step_size = 0.5

F32 = jnp.float32
BF16 = jnp.bfloat16


def token_index(x, y_hi, y_lo, z_hi):
    return ((x * 4 + y_hi) * 2 + y_lo) * 2 + z_hi


NEAR = [
    [token_index(x, y_hi, y_lo, z_hi) for x in range(4) for y_lo in range(2)]
    for y_hi in range(4)
    for z_hi in range(2)
]
FAR = [
    [token_index(x, y_hi, y_lo, z_hi) for y_hi in range(4) for z_hi in range(2)]
    for x in range(4)
    for y_lo in range(2)
]

def token_pairs(move):
    places = [(x, h, l, z) for x in range(4) for h in range(4) for l in range(2) for z in range(2)]
    return [(token_index(*p), token_index(*move(*p))) for p in places]


def from_beside(array):
    return lax.ppermute(array, "tokens", token_pairs(lambda x, h, l, z: (x, h, 1 - l, z)))


def from_along(array, steps):
    pairs = token_pairs(lambda x, h, l, z: ((x + steps) % 4, h, l, z))
    return lax.ppermute(array, "tokens", pairs)


def exchange(array, groups):
    return lax.all_to_all(array, "tokens", 0, 0, axis_index_groups=groups, tiled=True)


def mm(a, b, ca=1, cb=0):
    return lax.dot_general(a, b, (((ca,), (cb,)), ((), ())), preferred_element_type=F32)


def call(body, out_shape, *args, flops=0, scratch=(), space=pltpu.VMEM, limit=30):
    outs = out_shape if isinstance(out_shape, (tuple, list)) else [out_shape]
    moved = sum(a.size * a.dtype.itemsize for a in (*args, *outs))
    return pl.pallas_call(
        body,
        out_shape=out_shape,
        in_specs=[
            pl.BlockSpec(memory_space=pltpu.SMEM if a.dtype == jnp.int32 else space) for a in args
        ],
        out_specs=jax.tree.map(lambda _: pl.BlockSpec(memory_space=pltpu.VMEM), out_shape),
        scratch_shapes=list(scratch),
        compiler_params=pltpu.CompilerParams(vmem_limit_bytes=limit * 2**20),
        cost_estimate=pl.CostEstimate(flops=flops, bytes_accessed=moved, transcendentals=0),
    )(*args)


def scale_rows(rate_row, rows):
    tall = jnp.transpose(jnp.broadcast_to(rate_row, (128, rate_row.shape[1])))
    return (jnp.concatenate([tall, tall], axis=1) * rows.astype(F32)).astype(BF16)


def elementwise(gate, up, back):
    sig = jax.nn.sigmoid(gate)
    hidden = (gate * sig * up).astype(BF16)
    grad_gate = (back * up * sig * (1.0 + gate * (1.0 - sig))).astype(BF16)
    grad_up = (back * gate * sig).astype(BF16)
    return hidden, grad_gate, grad_up


def put_grads(out_ref, which, grad):
    grad = grad.astype(BF16)
    done = 0
    while done < DH:
        row = which * DH + done
        peer, inside = row // SHARE, row % SHARE
        count = min(SHARE - inside, DH - done)
        out_ref[peer, pl.ds(inside, count)] = grad[done : done + count]
        done += count


def local_grads(keys, scaled, gate_w, up_w, down_w, grads_ref):
    gate, up, back = mm(keys, gate_w), mm(keys, up_w), mm(scaled, down_w, 1, 1)
    hidden, grad_gate, grad_up = elementwise(gate, up, back)
    put_grads(grads_ref, 0, mm(keys, grad_gate, 0, 0))
    put_grads(grads_ref, 1, mm(keys, grad_up, 0, 0))
    put_grads(grads_ref, 2, mm(hidden, scaled, 0, 0))


def first_kernel(k_hbm, v_hbm, r_hbm, w_hbm, grads_ref, ahead_ref, k_ref, v_ref, r_ref, w_ref, sems):
    pairs = ((w_hbm, w_ref), (k_hbm, k_ref), (v_hbm, v_ref), (r_hbm, r_ref))
    copies = [pltpu.make_async_copy(a, b, sems.at[n]) for n, (a, b) in enumerate(pairs)]
    for copy in copies:
        copy.start()
    for copy in copies:
        copy.wait()
    scaled = scale_rows(r_ref[0], v_ref[0])
    local_grads(k_ref[0], scaled, w_ref[0, 0], w_ref[0, 1], w_ref[0, 2], grads_ref)
    ahead_ref[0] = k_ref[1]
    ahead_ref[1] = scale_rows(r_ref[1], v_ref[1])


def share_kernel(parts_ref, copies_ref):
    total = parts_ref[0].astype(F32)
    for peer in range(1, parts_ref.shape[0]):
        total = total + parts_ref[peer].astype(F32)
    total = total.astype(BF16)
    for peer in range(copies_ref.shape[0]):
        copies_ref[peer] = total


def newton_update(stacked, w_ref):
    current = []
    for m in range(3):
        wide = stacked[m].astype(F32)
        square = jnp.sum(jnp.sum(wide * wide, axis=0, keepdims=True), axis=1, keepdims=True)
        current.append((wide / (jnp.sqrt(square) + 1e-07)).astype(BF16))
    for step in range(NS_STEPS):
        grams = [mm(x, x, 1, 1).astype(BF16) for x in current]
        squares = [mm(a, a) for a in grams]
        mixers = [
            (coef_b * a.astype(F32) + coef_c * s).astype(BF16) for a, s in zip(grams, squares)
        ]
        products = [mm(b, x) for b, x in zip(mixers, current)]
        current = [(coef_a * x.astype(F32) + p).astype(BF16) for x, p in zip(current, products)]
    return [
        (w_ref[0, m].astype(F32) + step_size * current[m].astype(F32)).astype(BF16)
        for m in range(3)
    ]


def middle_kernel(grads_ref, w_ref, place_ref, *refs):
    tokens, (fresh_ref, out_ref, gate_ref, up_ref) = refs[:4], refs[4:]
    fresh = newton_update(grads_ref[...].reshape(3, DH, DH), w_ref)
    for m in range(3):
        fresh_ref[0, m] = fresh[m]
    gate_ref[...] = jnp.transpose(fresh[0])
    up_ref[...] = jnp.transpose(fresh[1])
    units = pl.ds(pl.multiple_of(place_ref[0] * UNITS, UNITS), UNITS)
    gate_w, up_w, down_w = gate_ref[units], up_ref[units], fresh_ref[0, 2, units]
    sums = [jnp.zeros((UNITS, DH), F32)] * 3
    for token_ref in tokens:
        keys = token_ref[:, 0].reshape(256, DH)
        scaled = token_ref[:, 1].reshape(256, DH)
        gate = mm(gate_w, keys, 1, 1)
        up = mm(up_w, keys, 1, 1)
        back = mm(down_w, scaled, 1, 1)
        hidden, grad_gate, grad_up = elementwise(gate, up, back)
        terms = mm(grad_gate, keys), mm(grad_up, keys), mm(hidden, scaled)
        sums = [s + t for s, t in zip(sums, terms)]
    for m in range(3):
        part = sums[m].astype(BF16)
        for peer in range(PEERS):
            out_ref[peer, pl.ds(m * UNITS, UNITS)] = part


def last_kernel(grads_ref, w_ref, fresh_ref):
    rows = [grads_ref[:, m * UNITS : (m + 1) * UNITS].reshape(DH, DH) for m in range(3)]
    stacked = [jnp.transpose(rows[0]), jnp.transpose(rows[1]), rows[2]]
    fresh = newton_update(stacked, w_ref)
    for m in range(3):
        fresh_ref[0, m] = fresh[m]


def query_kernel(q_ref, w0_ref, w1_ref, gain_ref, y_ref, squares_ref):
    for block, w_ref in enumerate((w0_ref, w1_ref)):
        gate = mm(q_ref[block], w_ref[0, 0])
        up = mm(q_ref[block], w_ref[0, 1])
        hidden = (gate * jax.nn.sigmoid(gate) * up).astype(BF16)
        out = mm(hidden, w_ref[0, 2])
        y_ref[block] = out * gain_ref[...]
        sums = jnp.sum(out * out, axis=1, keepdims=True)
        squares_ref[pl.ds(block, 1)] = jnp.transpose(jnp.broadcast_to(sums, (128, 128)))[:1]


def finish_kernel(y_ref, squares_ref, out_ref):
    root = jnp.sqrt(squares_ref[...] / D + 1e-06)
    for block in range(2):
        tall = jnp.transpose(jnp.broadcast_to(root[block : block + 1], (128, 128)))
        both = jnp.concatenate([tall, tall], axis=1)
        out_ref[block] = (y_ref[block] / both).astype(BF16)


def shaped(shape, dtype=BF16):
    return jax.ShapeDtypeStruct(shape, dtype)


def add_partner(squares, bit):
    pairs = [(h, h ^ bit) for h in range(8)]
    return squares + lax.ppermute(squares, "heads", pairs)


def together(*values):
    return lax.optimization_barrier(values)


def per_device(queries, keys, values, rates, fast_init, out_gain):
    pieces = shaped((PEERS, SHARE, DH))
    weights = shaped((1, 3, DH, DH))
    copied = [(2, 128, DH), (2, 128, DH), (2, 1, 128), (1, 3, DH, DH)]
    own = [pltpu.VMEM(shape, F32 if shape[1] == 1 else BF16) for shape in copied]
    grads, ahead = call(
        first_kernel, (pieces, shaped((2, 128, DH))), keys, values, rates, fast_init, flops=10**8,
        scratch=[*own, pltpu.SemaphoreType.DMA((4,))], space=pl.ANY, limit=58,
    )
    parts, beside = together(exchange(grads, NEAR), from_beside(ahead))
    shares = call(share_kernel, pieces, parts)
    shares, pair = together(shares, jnp.stack([ahead, beside]))
    parts, first = together(exchange(shares, FAR), from_along(pair, 2))
    others = [first, from_along(pair, 1), from_along(pair, 3)]
    whole = exchange(call(share_kernel, pieces, parts), NEAR)
    token = lax.axis_index("tokens")
    place = (token // 16 * 2 + token // 2 % 2).reshape(1)
    fresh, shares = call(
        middle_kernel, (weights, pieces), whole, fast_init, place, pair, *others, flops=9 * 10**8,
        scratch=[pltpu.VMEM((DH, DH), BF16)] * 2,
    )
    y, squares = call(
        query_kernel,
        (shaped((2, 128, DH), F32), shaped((2, 128), F32)),
        queries, fast_init, fresh, out_gain.reshape(1, DH), flops=10**8,
    )
    parts, y, squares = together(exchange(shares, FAR), y, add_partner(squares, 1))
    whole = exchange(call(share_kernel, pieces, parts), NEAR)
    whole, squares = together(whole, add_partner(squares, 2))
    final = call(last_kernel, weights, whole, fresh, flops=6 * 10**8)
    final, squares = together(final, add_partner(squares, 4))
    mixed = call(finish_kernel, shaped((2, 128, DH)), y, squares)
    return mixed, final


def solution(mesh):
    in_specs = (
        P(None, "tokens", "heads"),
        P(None, "tokens", "heads"),
        P(None, "tokens", "heads"),
        P(None, "heads", "tokens"),
        P("heads", None, None, None),
        P("heads"),
    )
    out_specs = (P(None, "tokens", "heads"), P("heads", None, None, None))
    return jax.shard_map(
        per_device, mesh=mesh, in_specs=in_specs, out_specs=out_specs, check_vma=False
    )
```

```python
import jax
import jax.numpy as jnp
from jax import lax
from jax.experimental import pallas as pl
from jax.experimental.pallas import tpu as pltpu
from jax.sharding import PartitionSpec as P

D = 2048
DH = 256
NS_STEPS = 2
PEERS = 8
SHARE = 3 * DH // PEERS
UNITS = DH // PEERS

coef_a = 3.4445
coef_b = -4.775
coef_c = 2.0315
step_size = 0.5

F32 = jnp.float32
BF16 = jnp.bfloat16


def token_index(x, y_hi, y_lo, z_hi):
    return ((x * 4 + y_hi) * 2 + y_lo) * 2 + z_hi


NEAR = [
    [token_index(x, y_hi, y_lo, z_hi) for x in range(4) for y_lo in range(2)]
    for y_hi in range(4)
    for z_hi in range(2)
]
FAR = [
    [token_index(x, y_hi, y_lo, z_hi) for y_hi in range(4) for z_hi in range(2)]
    for x in range(4)
    for y_lo in range(2)
]

def token_pairs(move):
    places = [(x, h, l, z) for x in range(4) for h in range(4) for l in range(2) for z in range(2)]
    return [(token_index(*p), token_index(*move(*p))) for p in places]


def from_beside(array):
    return lax.ppermute(array, "tokens", token_pairs(lambda x, h, l, z: (x, h, 1 - l, z)))


def from_along(array, steps):
    pairs = token_pairs(lambda x, h, l, z: ((x + steps) % 4, h, l, z))
    return lax.ppermute(array, "tokens", pairs)


def exchange(array, groups):
    return lax.all_to_all(array, "tokens", 0, 0, axis_index_groups=groups, tiled=True)


def mm(a, b, ca=1, cb=0):
    return lax.dot_general(a, b, (((ca,), (cb,)), ((), ())), preferred_element_type=F32)


def call(body, out_shape, *args, flops=0, scratch=(), space=pltpu.VMEM, limit=30):
    outs = out_shape if isinstance(out_shape, (tuple, list)) else [out_shape]
    moved = sum(a.size * a.dtype.itemsize for a in (*args, *outs))
    return pl.pallas_call(
        body,
        out_shape=out_shape,
        in_specs=[
            pl.BlockSpec(memory_space=pltpu.SMEM if a.dtype == jnp.int32 else space) for a in args
        ],
        out_specs=jax.tree.map(lambda _: pl.BlockSpec(memory_space=pltpu.VMEM), out_shape),
        scratch_shapes=list(scratch),
        compiler_params=pltpu.CompilerParams(vmem_limit_bytes=limit * 2**20),
        cost_estimate=pl.CostEstimate(flops=flops, bytes_accessed=moved, transcendentals=0),
    )(*args)


def scale_rows(rate_row, rows):
    tall = jnp.transpose(jnp.broadcast_to(rate_row, (128, rate_row.shape[1])))
    return (jnp.concatenate([tall, tall], axis=1) * rows.astype(F32)).astype(BF16)


def elementwise(gate, up, back):
    sig = jax.nn.sigmoid(gate)
    hidden = (gate * sig * up).astype(BF16)
    grad_gate = (back * up * sig * (1.0 + gate * (1.0 - sig))).astype(BF16)
    grad_up = (back * gate * sig).astype(BF16)
    return hidden, grad_gate, grad_up


def put_grads(out_ref, which, grad):
    grad = grad.astype(BF16)
    done = 0
    while done < DH:
        row = which * DH + done
        peer, inside = row // SHARE, row % SHARE
        count = min(SHARE - inside, DH - done)
        out_ref[peer, pl.ds(inside, count)] = grad[done : done + count]
        done += count


def local_grads(keys, scaled, gate_w, up_w, down_w, grads_ref):
    gate, up, back = mm(keys, gate_w), mm(keys, up_w), mm(scaled, down_w, 1, 1)
    hidden, grad_gate, grad_up = elementwise(gate, up, back)
    put_grads(grads_ref, 0, mm(keys, grad_gate, 0, 0))
    put_grads(grads_ref, 1, mm(keys, grad_up, 0, 0))
    put_grads(grads_ref, 2, mm(hidden, scaled, 0, 0))


def first_kernel(k_hbm, v_hbm, r_hbm, w_hbm, grads_ref, ahead_ref, k_ref, v_ref, r_ref, w_ref, sems):
    pairs = ((w_hbm, w_ref), (k_hbm, k_ref), (v_hbm, v_ref), (r_hbm, r_ref))
    copies = [pltpu.make_async_copy(a, b, sems.at[n]) for n, (a, b) in enumerate(pairs)]
    for copy in copies:
        copy.start()
    for copy in copies:
        copy.wait()
    scaled = scale_rows(r_ref[0], v_ref[0])
    local_grads(k_ref[0], scaled, w_ref[0, 0], w_ref[0, 1], w_ref[0, 2], grads_ref)
    ahead_ref[0] = k_ref[1]
    ahead_ref[1] = scale_rows(r_ref[1], v_ref[1])


def share_kernel(parts_ref, copies_ref):
    total = parts_ref[0].astype(F32)
    for peer in range(1, parts_ref.shape[0]):
        total = total + parts_ref[peer].astype(F32)
    total = total.astype(BF16)
    for peer in range(copies_ref.shape[0]):
        copies_ref[peer] = total


def newton_update(stacked, w_ref):
    current = []
    for m in range(3):
        wide = stacked[m].astype(F32)
        square = jnp.sum(jnp.sum(wide * wide, axis=0, keepdims=True), axis=1, keepdims=True)
        current.append((wide / (jnp.sqrt(square) + 1e-07)).astype(BF16))
    for step in range(NS_STEPS):
        grams = [mm(x, x, 1, 1).astype(BF16) for x in current]
        squares = [mm(a, a) for a in grams]
        mixers = [
            (coef_b * a.astype(F32) + coef_c * s).astype(BF16) for a, s in zip(grams, squares)
        ]
        products = [mm(b, x) for b, x in zip(mixers, current)]
        current = [(coef_a * x.astype(F32) + p).astype(BF16) for x, p in zip(current, products)]
    return [
        (w_ref[0, m].astype(F32) + step_size * current[m].astype(F32)).astype(BF16)
        for m in range(3)
    ]


def middle_kernel(grads_ref, w_ref, place_ref, *refs):
    tokens, (fresh_ref, out_ref, gate_ref, up_ref) = refs[:4], refs[4:]
    fresh = newton_update(grads_ref[...].reshape(3, DH, DH), w_ref)
    for m in range(3):
        fresh_ref[0, m] = fresh[m]
    gate_ref[...] = jnp.transpose(fresh[0])
    up_ref[...] = jnp.transpose(fresh[1])
    units = pl.ds(pl.multiple_of(place_ref[0] * UNITS, UNITS), UNITS)
    gate_w, up_w, down_w = gate_ref[units], up_ref[units], fresh_ref[0, 2, units]
    sums = [jnp.zeros((UNITS, DH), F32)] * 3
    for token_ref in tokens:
        keys = token_ref[:, 0].reshape(256, DH)
        scaled = token_ref[:, 1].reshape(256, DH)
        gate = mm(gate_w, keys, 1, 1)
        up = mm(up_w, keys, 1, 1)
        back = mm(down_w, scaled, 1, 1)
        hidden, grad_gate, grad_up = elementwise(gate, up, back)
        terms = mm(grad_gate, keys), mm(grad_up, keys), mm(hidden, scaled)
        sums = [s + t for s, t in zip(sums, terms)]
    for m in range(3):
        part = sums[m].astype(BF16)
        for peer in range(PEERS):
            out_ref[peer, pl.ds(m * UNITS, UNITS)] = part


def last_kernel(grads_ref, w_ref, fresh_ref):
    rows = [grads_ref[:, m * UNITS : (m + 1) * UNITS].reshape(DH, DH) for m in range(3)]
    stacked = [jnp.transpose(rows[0]), jnp.transpose(rows[1]), rows[2]]
    fresh = newton_update(stacked, w_ref)
    for m in range(3):
        fresh_ref[0, m] = fresh[m]


def query_kernel(q_ref, w0_ref, w1_ref, gain_ref, y_ref, squares_ref):
    for block, w_ref in enumerate((w0_ref, w1_ref)):
        gate = mm(q_ref[block], w_ref[0, 0])
        up = mm(q_ref[block], w_ref[0, 1])
        hidden = (gate * jax.nn.sigmoid(gate) * up).astype(BF16)
        out = mm(hidden, w_ref[0, 2])
        y_ref[block] = out * gain_ref[...]
        sums = jnp.sum(out * out, axis=1, keepdims=True)
        squares_ref[pl.ds(block, 1)] = jnp.transpose(jnp.broadcast_to(sums, (128, 128)))[:1]


def finish_kernel(y_ref, squares_ref, out_ref):
    root = jnp.sqrt(squares_ref[...] / D + 1e-06)
    for block in range(2):
        tall = jnp.transpose(jnp.broadcast_to(root[block : block + 1], (128, 128)))
        both = jnp.concatenate([tall, tall], axis=1)
        out_ref[block] = (y_ref[block] / both).astype(BF16)


def shaped(shape, dtype=BF16):
    return jax.ShapeDtypeStruct(shape, dtype)


def add_partner(squares, bit):
    pairs = [(h, h ^ bit) for h in range(8)]
    return squares + lax.ppermute(squares, "heads", pairs)


def together(*values):
    return lax.optimization_barrier(values)


def per_device(queries, keys, values, rates, fast_init, out_gain):
    pieces = shaped((PEERS, SHARE, DH))
    weights = shaped((1, 3, DH, DH))
    copied = [(2, 128, DH), (2, 128, DH), (2, 1, 128), (1, 3, DH, DH)]
    own = [pltpu.VMEM(shape, F32 if shape[1] == 1 else BF16) for shape in copied]
    grads, ahead = call(
        first_kernel, (pieces, shaped((2, 128, DH))), keys, values, rates, fast_init, flops=10**8,
        scratch=[*own, pltpu.SemaphoreType.DMA((4,))], space=pl.ANY, limit=58,
    )
    token = lax.axis_index("tokens")
    place = (token // 16 * 2 + token // 2 % 2).reshape(1)
    grads, place = together(grads, place)
    parts, beside = together(exchange(grads, NEAR), from_beside(ahead))
    shares = call(share_kernel, pieces, parts)
    shares, pair = together(shares, jnp.stack([ahead, beside]))
    parts, *others = together(
        exchange(shares, FAR), *(from_along(pair, steps) for steps in (1, 3, 2))
    )
    whole = exchange(call(share_kernel, pieces, parts), NEAR)
    fresh, shares = call(
        middle_kernel, (weights, pieces), whole, fast_init, place, pair, *others, flops=9 * 10**8,
        scratch=[pltpu.VMEM((DH, DH), BF16)] * 2,
    )
    y, squares = call(
        query_kernel,
        (shaped((2, 128, DH), F32), shaped((2, 128), F32)),
        queries, fast_init, fresh, out_gain.reshape(1, DH), flops=10**8,
    )
    squares = add_partner(add_partner(squares, 1), 2)
    parts, y, squares = together(exchange(shares, FAR), y, squares)
    whole = exchange(call(share_kernel, pieces, parts), NEAR)
    final = call(last_kernel, weights, whole, fresh, flops=6 * 10**8)
    squares = add_partner(squares, 4)
    mixed = call(finish_kernel, shaped((2, 128, DH)), y, squares)
    return mixed, final


def solution(mesh):
    in_specs = (
        P(None, "tokens", "heads"),
        P(None, "tokens", "heads"),
        P(None, "tokens", "heads"),
        P(None, "heads", "tokens"),
        P("heads", None, None, None),
        P("heads"),
    )
    out_specs = (P(None, "tokens", "heads"), P("heads", None, None, None))
    return jax.shard_map(
        per_device, mesh=mesh, in_specs=in_specs, out_specs=out_specs, check_vma=False
    )
```

```python
import jax
import jax.numpy as jnp
from jax import lax
from jax.experimental import pallas as pl
from jax.experimental.pallas import tpu as pltpu
from jax.sharding import PartitionSpec as P

D = 2048
DH = 256
NS_STEPS = 2
PEERS = 8
SHARE = 3 * DH // PEERS
UNITS = DH // PEERS

coef_a = 3.4445
coef_b = -4.775
coef_c = 2.0315
step_size = 0.5

F32 = jnp.float32
BF16 = jnp.bfloat16


def token_index(x, y_hi, y_lo, z_hi):
    return ((x * 4 + y_hi) * 2 + y_lo) * 2 + z_hi


NEAR = [
    [token_index(x, y_hi, y_lo, z_hi) for x in range(4) for y_lo in range(2)]
    for y_hi in range(4)
    for z_hi in range(2)
]
FAR = [
    [token_index(x, y_hi, y_lo, z_hi) for y_hi in range(4) for z_hi in range(2)]
    for x in range(4)
    for y_lo in range(2)
]

def token_pairs(move):
    places = [(x, h, l, z) for x in range(4) for h in range(4) for l in range(2) for z in range(2)]
    return [(token_index(*p), token_index(*move(*p))) for p in places]


def from_beside(array):
    return lax.ppermute(array, "tokens", token_pairs(lambda x, h, l, z: (x, h, 1 - l, z)))


def from_along(array, steps):
    pairs = token_pairs(lambda x, h, l, z: ((x + steps) % 4, h, l, z))
    return lax.ppermute(array, "tokens", pairs)


def exchange(array, groups):
    return lax.all_to_all(array, "tokens", 0, 0, axis_index_groups=groups, tiled=True)


def mm(a, b, ca=1, cb=0):
    return lax.dot_general(a, b, (((ca,), (cb,)), ((), ())), preferred_element_type=F32)


def call(body, out_shape, *args, flops=0, scratch=(), space=pltpu.VMEM, limit=30):
    outs = out_shape if isinstance(out_shape, (tuple, list)) else [out_shape]
    moved = sum(a.size * a.dtype.itemsize for a in (*args, *outs))
    return pl.pallas_call(
        body,
        out_shape=out_shape,
        in_specs=[
            pl.BlockSpec(memory_space=pltpu.SMEM if a.dtype == jnp.int32 else space) for a in args
        ],
        out_specs=jax.tree.map(lambda _: pl.BlockSpec(memory_space=pltpu.VMEM), out_shape),
        scratch_shapes=list(scratch),
        compiler_params=pltpu.CompilerParams(vmem_limit_bytes=limit * 2**20),
        cost_estimate=pl.CostEstimate(flops=flops, bytes_accessed=moved, transcendentals=0),
    )(*args)


def scale_rows(rate_row, rows):
    tall = jnp.transpose(jnp.broadcast_to(rate_row, (128, rate_row.shape[1])))
    return (jnp.concatenate([tall, tall], axis=1) * rows.astype(F32)).astype(BF16)


def elementwise(gate, up, back):
    sig = jax.nn.sigmoid(gate)
    hidden = (gate * sig * up).astype(BF16)
    grad_gate = (back * up * sig * (1.0 + gate * (1.0 - sig))).astype(BF16)
    grad_up = (back * gate * sig).astype(BF16)
    return hidden, grad_gate, grad_up


def put_grads(out_ref, which, grad):
    grad = grad.astype(BF16)
    done = 0
    while done < DH:
        row = which * DH + done
        peer, inside = row // SHARE, row % SHARE
        count = min(SHARE - inside, DH - done)
        out_ref[peer, pl.ds(inside, count)] = grad[done : done + count]
        done += count


def local_grads(keys, scaled, gate_w, up_w, down_w, grads_ref):
    gate, up, back = mm(keys, gate_w), mm(keys, up_w), mm(scaled, down_w, 1, 1)
    hidden, grad_gate, grad_up = elementwise(gate, up, back)
    put_grads(grads_ref, 0, mm(keys, grad_gate, 0, 0))
    put_grads(grads_ref, 1, mm(keys, grad_up, 0, 0))
    put_grads(grads_ref, 2, mm(hidden, scaled, 0, 0))


def first_kernel(k_hbm, v_hbm, r_hbm, w_hbm, grads_ref, ahead_ref, k_ref, v_ref, r_ref, w_ref, sems):
    pairs = ((w_hbm, w_ref), (k_hbm, k_ref), (v_hbm, v_ref), (r_hbm, r_ref))
    copies = [pltpu.make_async_copy(a, b, sems.at[n]) for n, (a, b) in enumerate(pairs)]
    for copy in copies:
        copy.start()
    for copy in copies:
        copy.wait()
    scaled = scale_rows(r_ref[0], v_ref[0])
    local_grads(k_ref[0], scaled, w_ref[0, 0], w_ref[0, 1], w_ref[0, 2], grads_ref)
    ahead_ref[0] = k_ref[1]
    ahead_ref[1] = scale_rows(r_ref[1], v_ref[1])


def share_kernel(parts_ref, copies_ref):
    total = parts_ref[0].astype(F32)
    for peer in range(1, parts_ref.shape[0]):
        total = total + parts_ref[peer].astype(F32)
    total = total.astype(BF16)
    for peer in range(copies_ref.shape[0]):
        copies_ref[peer] = total


def newton_update(stacked, w_ref):
    current = []
    for m in range(3):
        wide = stacked[m].astype(F32)
        square = jnp.sum(jnp.sum(wide * wide, axis=0, keepdims=True), axis=1, keepdims=True)
        current.append((wide / (jnp.sqrt(square) + 1e-07)).astype(BF16))
    for step in range(NS_STEPS):
        grams = [mm(x, x, 1, 1).astype(BF16) for x in current]
        squares = [mm(a, a) for a in grams]
        mixers = [
            (coef_b * a.astype(F32) + coef_c * s).astype(BF16) for a, s in zip(grams, squares)
        ]
        products = [mm(b, x) for b, x in zip(mixers, current)]
        current = [(coef_a * x.astype(F32) + p).astype(BF16) for x, p in zip(current, products)]
    return [
        (w_ref[0, m].astype(F32) + step_size * current[m].astype(F32)).astype(BF16)
        for m in range(3)
    ]


def middle_kernel(grads_ref, w_ref, place_ref, *refs):
    tokens, (fresh_ref, out_ref, gate_ref, up_ref) = refs[:4], refs[4:]
    fresh = newton_update(grads_ref[...].reshape(3, DH, DH), w_ref)
    for m in range(3):
        fresh_ref[0, m] = fresh[m]
    gate_ref[...] = jnp.transpose(fresh[0])
    up_ref[...] = jnp.transpose(fresh[1])
    units = pl.ds(pl.multiple_of(place_ref[0] * UNITS, UNITS), UNITS)
    gate_w, up_w, down_w = gate_ref[units], up_ref[units], fresh_ref[0, 2, units]
    sums = [jnp.zeros((UNITS, DH), F32)] * 3
    for token_ref in tokens:
        keys = token_ref[:, 0].reshape(256, DH)
        scaled = token_ref[:, 1].reshape(256, DH)
        gate = mm(gate_w, keys, 1, 1)
        up = mm(up_w, keys, 1, 1)
        back = mm(down_w, scaled, 1, 1)
        hidden, grad_gate, grad_up = elementwise(gate, up, back)
        terms = mm(grad_gate, keys), mm(grad_up, keys), mm(hidden, scaled)
        sums = [s + t for s, t in zip(sums, terms)]
    for m in range(3):
        part = sums[m].astype(BF16)
        for peer in range(PEERS):
            out_ref[peer, pl.ds(m * UNITS, UNITS)] = part


def last_kernel(grads_ref, w_ref, fresh_ref):
    rows = [grads_ref[:, m * UNITS : (m + 1) * UNITS].reshape(DH, DH) for m in range(3)]
    stacked = [jnp.transpose(rows[0]), jnp.transpose(rows[1]), rows[2]]
    fresh = newton_update(stacked, w_ref)
    for m in range(3):
        fresh_ref[0, m] = fresh[m]


def query_kernel(q_ref, w0_ref, w1_ref, gain_ref, y_ref, squares_ref):
    for block, w_ref in enumerate((w0_ref, w1_ref)):
        gate = mm(q_ref[block], w_ref[0, 0])
        up = mm(q_ref[block], w_ref[0, 1])
        hidden = (gate * jax.nn.sigmoid(gate) * up).astype(BF16)
        out = mm(hidden, w_ref[0, 2])
        y_ref[block] = out * gain_ref[...]
        sums = jnp.sum(out * out, axis=1, keepdims=True)
        squares_ref[pl.ds(block, 1)] = jnp.transpose(jnp.broadcast_to(sums, (128, 128)))[:1]


def finish_kernel(y_ref, squares_ref, out_ref):
    root = jnp.sqrt(squares_ref[...] / D + 1e-06)
    for block in range(2):
        tall = jnp.transpose(jnp.broadcast_to(root[block : block + 1], (128, 128)))
        both = jnp.concatenate([tall, tall], axis=1)
        out_ref[block] = (y_ref[block] / both).astype(BF16)


def shaped(shape, dtype=BF16):
    return jax.ShapeDtypeStruct(shape, dtype)


def add_partner(squares, bit):
    pairs = [(h, h ^ bit) for h in range(8)]
    return squares + lax.ppermute(squares, "heads", pairs)


def together(*values):
    return lax.optimization_barrier(values)


def per_device(queries, keys, values, rates, fast_init, out_gain):
    pieces = shaped((PEERS, SHARE, DH))
    weights = shaped((1, 3, DH, DH))
    copied = [(2, 128, DH), (2, 128, DH), (2, 1, 128), (1, 3, DH, DH)]
    own = [pltpu.VMEM(shape, F32 if shape[1] == 1 else BF16) for shape in copied]
    grads, ahead = call(
        first_kernel, (pieces, shaped((2, 128, DH))), keys, values, rates, fast_init, flops=10**8,
        scratch=[*own, pltpu.SemaphoreType.DMA((4,))], space=pl.ANY, limit=58,
    )
    token = lax.axis_index("tokens")
    place = (token // 16 * 2 + token // 2 % 2).reshape(1)
    grads, place = together(grads, place)
    parts, beside = together(exchange(grads, NEAR), from_beside(ahead))
    shares = call(share_kernel, pieces, parts)
    shares, pair = together(shares, jnp.stack([ahead, beside]))
    parts, *others = together(
        exchange(shares, FAR), *(from_along(pair, steps) for steps in (1, 3, 2))
    )
    whole = exchange(call(share_kernel, pieces, parts), NEAR)
    fresh, shares = call(
        middle_kernel, (weights, pieces), whole, fast_init, place, pair, *others, flops=9 * 10**8,
        scratch=[pltpu.VMEM((DH, DH), BF16)] * 2,
    )
    y, squares = call(
        query_kernel,
        (shaped((2, 128, DH), F32), shaped((2, 128), F32)),
        queries, fast_init, fresh, out_gain.reshape(1, DH), flops=10**8,
    )
    squares = add_partner(add_partner(squares, 2), 4)
    parts, y, squares = together(exchange(shares, FAR), y, squares)
    whole = exchange(call(share_kernel, pieces, parts), NEAR)
    final = call(last_kernel, weights, whole, fresh, flops=6 * 10**8)
    squares = add_partner(squares, 1)
    mixed = call(finish_kernel, shaped((2, 128, DH)), y, squares)
    return mixed, final


def solution(mesh):
    in_specs = (
        P(None, "tokens", "heads"),
        P(None, "tokens", "heads"),
        P(None, "tokens", "heads"),
        P(None, "heads", "tokens"),
        P("heads", None, None, None),
        P("heads"),
    )
    out_specs = (P(None, "tokens", "heads"), P("heads", None, None, None))
    return jax.shard_map(
        per_device, mesh=mesh, in_specs=in_specs, out_specs=out_specs, check_vma=False
    )
```

```python
import jax
import jax.numpy as jnp
from jax import lax
from jax.experimental import pallas as pl
from jax.experimental.pallas import tpu as pltpu
from jax.sharding import PartitionSpec as P

D = 2048
DH = 256
NS_STEPS = 2
PEERS = 8
SHARE = 3 * DH // PEERS
UNITS = DH // PEERS

coef_a = 3.4445
coef_b = -4.775
coef_c = 2.0315
step_size = 0.5

F32 = jnp.float32
BF16 = jnp.bfloat16


def token_index(x, y_hi, y_lo, z_hi):
    return ((x * 4 + y_hi) * 2 + y_lo) * 2 + z_hi


NEAR = [
    [token_index(x, y_hi, y_lo, z_hi) for x in range(4) for y_lo in range(2)]
    for y_hi in range(4)
    for z_hi in range(2)
]
FAR = [
    [token_index(x, y_hi, y_lo, z_hi) for y_hi in range(4) for z_hi in range(2)]
    for x in range(4)
    for y_lo in range(2)
]

def token_pairs(move):
    places = [(x, h, l, z) for x in range(4) for h in range(4) for l in range(2) for z in range(2)]
    return [(token_index(*p), token_index(*move(*p))) for p in places]


def from_beside(array):
    return lax.ppermute(array, "tokens", token_pairs(lambda x, h, l, z: (x, h, 1 - l, z)))


def from_along(array, steps):
    pairs = token_pairs(lambda x, h, l, z: ((x + steps) % 4, h, l, z))
    return lax.ppermute(array, "tokens", pairs)


def exchange(array, groups):
    return lax.all_to_all(array, "tokens", 0, 0, axis_index_groups=groups, tiled=True)


def mm(a, b, ca=1, cb=0):
    return lax.dot_general(a, b, (((ca,), (cb,)), ((), ())), preferred_element_type=F32)


def call(body, out_shape, *args, flops=0, scratch=(), space=pltpu.VMEM, limit=30):
    outs = out_shape if isinstance(out_shape, (tuple, list)) else [out_shape]
    moved = sum(a.size * a.dtype.itemsize for a in (*args, *outs))
    return pl.pallas_call(
        body,
        out_shape=out_shape,
        in_specs=[
            pl.BlockSpec(memory_space=pltpu.SMEM if a.dtype == jnp.int32 else space) for a in args
        ],
        out_specs=jax.tree.map(lambda _: pl.BlockSpec(memory_space=pltpu.VMEM), out_shape),
        scratch_shapes=list(scratch),
        compiler_params=pltpu.CompilerParams(vmem_limit_bytes=limit * 2**20),
        cost_estimate=pl.CostEstimate(flops=flops, bytes_accessed=moved, transcendentals=0),
    )(*args)


def scale_rows(rate_row, rows):
    tall = jnp.transpose(jnp.broadcast_to(rate_row, (128, rate_row.shape[1])))
    return (jnp.concatenate([tall, tall], axis=1) * rows.astype(F32)).astype(BF16)


def elementwise(gate, up, back):
    sig = jax.nn.sigmoid(gate)
    hidden = (gate * sig * up).astype(BF16)
    grad_gate = (back * up * sig * (1.0 + gate * (1.0 - sig))).astype(BF16)
    grad_up = (back * gate * sig).astype(BF16)
    return hidden, grad_gate, grad_up


def put_grads(out_ref, which, grad):
    grad = grad.astype(BF16)
    done = 0
    while done < DH:
        row = which * DH + done
        peer, inside = row // SHARE, row % SHARE
        count = min(SHARE - inside, DH - done)
        out_ref[peer, pl.ds(inside, count)] = grad[done : done + count]
        done += count


def local_grads(keys, scaled, gate_w, up_w, down_w, grads_ref):
    gate, up, back = mm(keys, gate_w), mm(keys, up_w), mm(scaled, down_w, 1, 1)
    hidden, grad_gate, grad_up = elementwise(gate, up, back)
    put_grads(grads_ref, 0, mm(keys, grad_gate, 0, 0))
    put_grads(grads_ref, 1, mm(keys, grad_up, 0, 0))
    put_grads(grads_ref, 2, mm(hidden, scaled, 0, 0))


def first_kernel(k_hbm, v_hbm, r_hbm, w_hbm, grads_ref, ahead_ref, k_ref, v_ref, r_ref, w_ref, sems):
    pairs = ((w_hbm, w_ref), (k_hbm, k_ref), (v_hbm, v_ref), (r_hbm, r_ref))
    copies = [pltpu.make_async_copy(a, b, sems.at[n]) for n, (a, b) in enumerate(pairs)]
    for copy in copies:
        copy.start()
    for copy in copies:
        copy.wait()
    scaled = scale_rows(r_ref[0], v_ref[0])
    local_grads(k_ref[0], scaled, w_ref[0, 0], w_ref[0, 1], w_ref[0, 2], grads_ref)
    ahead_ref[0] = k_ref[1]
    ahead_ref[1] = scale_rows(r_ref[1], v_ref[1])


def share_kernel(parts_ref, copies_ref):
    total = parts_ref[0].astype(F32)
    for peer in range(1, parts_ref.shape[0]):
        total = total + parts_ref[peer].astype(F32)
    total = total.astype(BF16)
    for peer in range(copies_ref.shape[0]):
        copies_ref[peer] = total


def newton_update(stacked, w_ref):
    current = []
    for m in range(3):
        wide = stacked[m].astype(F32)
        square = jnp.sum(jnp.sum(wide * wide, axis=0, keepdims=True), axis=1, keepdims=True)
        current.append((wide * (1.0 / (jnp.sqrt(square) + 1e-07))).astype(BF16))
    for step in range(NS_STEPS):
        grams = [mm(x, x, 1, 1).astype(BF16) for x in current]
        squares = [mm(a, a) for a in grams]
        mixers = [
            (coef_b * a.astype(F32) + coef_c * s).astype(BF16) for a, s in zip(grams, squares)
        ]
        products = [mm(b, x) for b, x in zip(mixers, current)]
        current = [(coef_a * x.astype(F32) + p).astype(BF16) for x, p in zip(current, products)]
    return [
        (w_ref[0, m].astype(F32) + step_size * current[m].astype(F32)).astype(BF16)
        for m in range(3)
    ]


def middle_kernel(grads_ref, w_ref, place_ref, *refs):
    tokens, (fresh_ref, out_ref, gate_ref, up_ref) = refs[:4], refs[4:]
    fresh = newton_update(grads_ref[...].reshape(3, DH, DH), w_ref)
    for m in range(3):
        fresh_ref[0, m] = fresh[m]
    gate_ref[...] = jnp.transpose(fresh[0])
    up_ref[...] = jnp.transpose(fresh[1])
    units = pl.ds(pl.multiple_of(place_ref[0] * UNITS, UNITS), UNITS)
    pair_w = jnp.concatenate([gate_ref[units], up_ref[units]], axis=0)
    down_w = fresh_ref[0, 2, units]
    pair_sum, down_sum = jnp.zeros((2 * UNITS, DH), F32), jnp.zeros((UNITS, DH), F32)
    for token_ref in tokens:
        keys = token_ref[:, 0].reshape(256, DH)
        scaled = token_ref[:, 1].reshape(256, DH)
        gate_up = mm(pair_w, keys, 1, 1)
        back = mm(down_w, scaled, 1, 1)
        hidden, grad_gate, grad_up = elementwise(gate_up[:UNITS], gate_up[UNITS:], back)
        pair_sum = pair_sum + mm(jnp.concatenate([grad_gate, grad_up], axis=0), keys)
        down_sum = down_sum + mm(hidden, scaled)
    sums = pair_sum[:UNITS], pair_sum[UNITS:], down_sum
    for m in range(3):
        part = sums[m].astype(BF16)
        for peer in range(PEERS):
            out_ref[peer, pl.ds(m * UNITS, UNITS)] = part


def last_kernel(grads_ref, w_ref, fresh_ref):
    rows = [grads_ref[:, m * UNITS : (m + 1) * UNITS].reshape(DH, DH) for m in range(3)]
    stacked = [jnp.transpose(rows[0]), jnp.transpose(rows[1]), rows[2]]
    fresh = newton_update(stacked, w_ref)
    for m in range(3):
        fresh_ref[0, m] = fresh[m]


def query_kernel(q_ref, w0_ref, w1_ref, gain_ref, y_ref, squares_ref):
    for block, w_ref in enumerate((w0_ref, w1_ref)):
        gate = mm(q_ref[block], w_ref[0, 0])
        up = mm(q_ref[block], w_ref[0, 1])
        hidden = (gate * jax.nn.sigmoid(gate) * up).astype(BF16)
        out = mm(hidden, w_ref[0, 2])
        y_ref[block] = out * gain_ref[...]
        sums = jnp.sum(out * out, axis=1, keepdims=True)
        squares_ref[pl.ds(block, 1)] = jnp.transpose(jnp.broadcast_to(sums, (128, 128)))[:1]


def finish_kernel(y_ref, squares_ref, out_ref):
    root = jnp.sqrt(squares_ref[...] / D + 1e-06)
    for block in range(2):
        tall = jnp.transpose(jnp.broadcast_to(root[block : block + 1], (128, 128)))
        both = jnp.concatenate([tall, tall], axis=1)
        out_ref[block] = (y_ref[block] / both).astype(BF16)


def shaped(shape, dtype=BF16):
    return jax.ShapeDtypeStruct(shape, dtype)


def add_partner(squares, bit):
    pairs = [(h, h ^ bit) for h in range(8)]
    return squares + lax.ppermute(squares, "heads", pairs)


def together(*values):
    return lax.optimization_barrier(values)


def per_device(queries, keys, values, rates, fast_init, out_gain):
    pieces = shaped((PEERS, SHARE, DH))
    weights = shaped((1, 3, DH, DH))
    copied = [(2, 128, DH), (2, 128, DH), (2, 1, 128), (1, 3, DH, DH)]
    own = [pltpu.VMEM(shape, F32 if shape[1] == 1 else BF16) for shape in copied]
    grads, ahead = call(
        first_kernel, (pieces, shaped((2, 128, DH))), keys, values, rates, fast_init, flops=10**8,
        scratch=[*own, pltpu.SemaphoreType.DMA((4,))], space=pl.ANY, limit=58,
    )
    token = lax.axis_index("tokens")
    place = (token // 16 * 2 + token // 2 % 2).reshape(1)
    grads, place = together(grads, place)
    parts, beside = together(exchange(grads, NEAR), from_beside(ahead))
    shares = call(share_kernel, pieces, parts)
    shares, pair = together(shares, jnp.stack([ahead, beside]))
    parts, *others = together(
        exchange(shares, FAR), *(from_along(pair, steps) for steps in (1, 3, 2))
    )
    whole = exchange(call(share_kernel, pieces, parts), NEAR)
    fresh, shares = call(
        middle_kernel, (weights, pieces), whole, fast_init, place, pair, *others, flops=9 * 10**8,
        scratch=[pltpu.VMEM((DH, DH), BF16)] * 2,
    )
    y, squares = call(
        query_kernel,
        (shaped((2, 128, DH), F32), shaped((2, 128), F32)),
        queries, fast_init, fresh, out_gain.reshape(1, DH), flops=10**8,
    )
    squares = add_partner(add_partner(squares, 2), 4)
    parts, y, squares = together(exchange(shares, FAR), y, squares)
    whole = exchange(call(share_kernel, pieces, parts), NEAR)
    final = call(last_kernel, weights, whole, fresh, flops=6 * 10**8)
    squares = add_partner(squares, 1)
    mixed = call(finish_kernel, shaped((2, 128, DH)), y, squares)
    return mixed, final


def solution(mesh):
    in_specs = (
        P(None, "tokens", "heads"),
        P(None, "tokens", "heads"),
        P(None, "tokens", "heads"),
        P(None, "heads", "tokens"),
        P("heads", None, None, None),
        P("heads"),
    )
    out_specs = (P(None, "tokens", "heads"), P("heads", None, None, None))
    return jax.shard_map(
        per_device, mesh=mesh, in_specs=in_specs, out_specs=out_specs, check_vma=False
    )
```

```python
import jax
import jax.numpy as jnp
from jax import lax
from jax.experimental import pallas as pl
from jax.experimental.pallas import tpu as pltpu
from jax.sharding import PartitionSpec as P

D = 2048
DH = 256
NS_STEPS = 2
PEERS = 8
SHARE = 3 * DH // PEERS
UNITS = DH // PEERS

coef_a = 3.4445
coef_b = -4.775
coef_c = 2.0315
step_size = 0.5

F32 = jnp.float32
BF16 = jnp.bfloat16


def token_index(x, y_hi, y_lo, z_hi):
    return ((x * 4 + y_hi) * 2 + y_lo) * 2 + z_hi


NEAR = [
    [token_index(x, y_hi, y_lo, z_hi) for x in range(4) for y_lo in range(2)]
    for y_hi in range(4)
    for z_hi in range(2)
]
FAR = [
    [token_index(x, y_hi, y_lo, z_hi) for y_hi in range(4) for z_hi in range(2)]
    for x in range(4)
    for y_lo in range(2)
]
LOOP = [
    [token_index(x, y_hi, y_lo, 0) for y_hi in range(4)]
    + [token_index(x, y_hi, y_lo, 1) for y_hi in reversed(range(4))]
    for x in range(4)
    for y_lo in range(2)
]


def token_pairs(move):
    places = [(x, h, l, z) for x in range(4) for h in range(4) for l in range(2) for z in range(2)]
    return [(token_index(*p), token_index(*move(*p))) for p in places]


def from_beside(array):
    return lax.ppermute(array, "tokens", token_pairs(lambda x, h, l, z: (x, h, 1 - l, z)))


def from_along(array, steps):
    pairs = token_pairs(lambda x, h, l, z: ((x + steps) % 4, h, l, z))
    return lax.ppermute(array, "tokens", pairs)


def exchange(array, groups):
    return lax.all_to_all(array, "tokens", 0, 0, axis_index_groups=groups, tiled=True)


def mm(a, b, ca=1, cb=0):
    return lax.dot_general(a, b, (((ca,), (cb,)), ((), ())), preferred_element_type=F32)


def call(body, out_shape, *args, flops=0, scratch=(), space=pltpu.VMEM, limit=30):
    outs = out_shape if isinstance(out_shape, (tuple, list)) else [out_shape]
    moved = sum(a.size * a.dtype.itemsize for a in (*args, *outs))
    return pl.pallas_call(
        body,
        out_shape=out_shape,
        in_specs=[
            pl.BlockSpec(memory_space=pltpu.SMEM if a.dtype == jnp.int32 else space) for a in args
        ],
        out_specs=jax.tree.map(lambda _: pl.BlockSpec(memory_space=pltpu.VMEM), out_shape),
        scratch_shapes=list(scratch),
        compiler_params=pltpu.CompilerParams(vmem_limit_bytes=limit * 2**20),
        cost_estimate=pl.CostEstimate(flops=flops, bytes_accessed=moved, transcendentals=0),
    )(*args)


def scale_rows(rate_row, rows):
    tall = jnp.transpose(jnp.broadcast_to(rate_row, (128, rate_row.shape[1])))
    return (jnp.concatenate([tall, tall], axis=1) * rows.astype(F32)).astype(BF16)


def elementwise(gate, up, back):
    sig = jax.nn.sigmoid(gate)
    hidden = (gate * sig * up).astype(BF16)
    grad_gate = (back * up * sig * (1.0 + gate * (1.0 - sig))).astype(BF16)
    grad_up = (back * gate * sig).astype(BF16)
    return hidden, grad_gate, grad_up


def put_grads(out_ref, which, grad):
    grad = grad.astype(BF16)
    done = 0
    while done < DH:
        row = which * DH + done
        peer, inside = row // SHARE, row % SHARE
        count = min(SHARE - inside, DH - done)
        out_ref[peer, pl.ds(inside, count)] = grad[done : done + count]
        done += count


def local_grads(keys, scaled, gate_w, up_w, down_w, grads_ref):
    gate, up, back = mm(keys, gate_w), mm(keys, up_w), mm(scaled, down_w, 1, 1)
    hidden, grad_gate, grad_up = elementwise(gate, up, back)
    put_grads(grads_ref, 0, mm(keys, grad_gate, 0, 0))
    put_grads(grads_ref, 1, mm(keys, grad_up, 0, 0))
    put_grads(grads_ref, 2, mm(hidden, scaled, 0, 0))


def first_kernel(k_hbm, v_hbm, r_hbm, w_hbm, grads_ref, ahead_ref, k_ref, v_ref, r_ref, w_ref, sems):
    pairs = ((w_hbm, w_ref), (k_hbm, k_ref), (v_hbm, v_ref), (r_hbm, r_ref))
    copies = [pltpu.make_async_copy(a, b, sems.at[n]) for n, (a, b) in enumerate(pairs)]
    for copy in copies:
        copy.start()
    for copy in copies:
        copy.wait()
    scaled = scale_rows(r_ref[0], v_ref[0])
    local_grads(k_ref[0], scaled, w_ref[0, 0], w_ref[0, 1], w_ref[0, 2], grads_ref)
    ahead_ref[0] = k_ref[1]
    ahead_ref[1] = scale_rows(r_ref[1], v_ref[1])


def share_kernel(parts_ref, copies_ref):
    total = parts_ref[0].astype(F32)
    for peer in range(1, parts_ref.shape[0]):
        total = total + parts_ref[peer].astype(F32)
    total = total.astype(BF16)
    for peer in range(copies_ref.shape[0]):
        copies_ref[peer] = total


def newton_update(stacked, w_ref):
    current = []
    for m in range(3):
        wide = stacked[m].astype(F32)
        square = jnp.sum(jnp.sum(wide * wide, axis=0, keepdims=True), axis=1, keepdims=True)
        current.append((wide * (1.0 / (jnp.sqrt(square) + 1e-07))).astype(BF16))
    for step in range(NS_STEPS):
        grams = [mm(x, x, 1, 1).astype(BF16) for x in current]
        squares = [mm(a, a) for a in grams]
        mixers = [
            (coef_b * a.astype(F32) + coef_c * s).astype(BF16) for a, s in zip(grams, squares)
        ]
        products = [mm(b, x) for b, x in zip(mixers, current)]
        current = [(coef_a * x.astype(F32) + p).astype(BF16) for x, p in zip(current, products)]
    return [
        (w_ref[0, m].astype(F32) + step_size * current[m].astype(F32)).astype(BF16)
        for m in range(3)
    ]


def middle_kernel(grads_ref, w_ref, place_ref, *refs):
    tokens, (fresh_ref, out_ref, gate_ref, up_ref) = refs[:4], refs[4:]
    fresh = newton_update(grads_ref[...].reshape(3, DH, DH), w_ref)
    for m in range(3):
        fresh_ref[0, m] = fresh[m]
    gate_ref[...] = jnp.transpose(fresh[0])
    up_ref[...] = jnp.transpose(fresh[1])
    units = pl.ds(pl.multiple_of(place_ref[0] * UNITS, UNITS), UNITS)
    pair_w = jnp.concatenate([gate_ref[units], up_ref[units]], axis=0)
    down_w = fresh_ref[0, 2, units]
    pair_sum, down_sum = jnp.zeros((2 * UNITS, DH), F32), jnp.zeros((UNITS, DH), F32)
    for token_ref in tokens:
        keys = token_ref[:, 0].reshape(256, DH)
        scaled = token_ref[:, 1].reshape(256, DH)
        gate_up = mm(pair_w, keys, 1, 1)
        back = mm(down_w, scaled, 1, 1)
        hidden, grad_gate, grad_up = elementwise(gate_up[:UNITS], gate_up[UNITS:], back)
        pair_sum = pair_sum + mm(jnp.concatenate([grad_gate, grad_up], axis=0), keys)
        down_sum = down_sum + mm(hidden, scaled)
    sums = pair_sum[:UNITS], pair_sum[UNITS:], down_sum
    for m in range(3):
        part = sums[m].astype(BF16)
        for peer in range(PEERS):
            out_ref[peer, pl.ds(m * UNITS, UNITS)] = part


def last_kernel(grads_ref, w_ref, fresh_ref):
    rows = [grads_ref[:, m * UNITS : (m + 1) * UNITS].reshape(DH, DH) for m in range(3)]
    stacked = [jnp.transpose(rows[0]), jnp.transpose(rows[1]), rows[2]]
    fresh = newton_update(stacked, w_ref)
    for m in range(3):
        fresh_ref[0, m] = fresh[m]


def query_kernel(q_ref, w0_ref, w1_ref, gain_ref, y_ref, squares_ref):
    for block, w_ref in enumerate((w0_ref, w1_ref)):
        gate = mm(q_ref[block], w_ref[0, 0])
        up = mm(q_ref[block], w_ref[0, 1])
        hidden = (gate * jax.nn.sigmoid(gate) * up).astype(BF16)
        out = mm(hidden, w_ref[0, 2])
        y_ref[block] = out * gain_ref[...]
        sums = jnp.sum(out * out, axis=1, keepdims=True)
        squares_ref[pl.ds(block, 1)] = jnp.transpose(jnp.broadcast_to(sums, (128, 128)))[:1]


def finish_kernel(y_ref, squares_ref, out_ref):
    root = jnp.sqrt(squares_ref[...] / D + 1e-06)
    for block in range(2):
        tall = jnp.transpose(jnp.broadcast_to(root[block : block + 1], (128, 128)))
        both = jnp.concatenate([tall, tall], axis=1)
        out_ref[block] = (y_ref[block] / both).astype(BF16)


def shaped(shape, dtype=BF16):
    return jax.ShapeDtypeStruct(shape, dtype)


def add_partner(squares, bit):
    pairs = [(h, h ^ bit) for h in range(8)]
    return squares + lax.ppermute(squares, "heads", pairs)


def together(*values):
    return lax.optimization_barrier(values)


def per_device(queries, keys, values, rates, fast_init, out_gain):
    pieces = shaped((PEERS, SHARE, DH))
    weights = shaped((1, 3, DH, DH))
    copied = [(2, 128, DH), (2, 128, DH), (2, 1, 128), (1, 3, DH, DH)]
    own = [pltpu.VMEM(shape, F32 if shape[1] == 1 else BF16) for shape in copied]
    grads, ahead = call(
        first_kernel, (pieces, shaped((2, 128, DH))), keys, values, rates, fast_init, flops=10**8,
        scratch=[*own, pltpu.SemaphoreType.DMA((4,))], space=pl.ANY, limit=58,
    )
    token = lax.axis_index("tokens")
    place = (token // 16 * 2 + token // 2 % 2).reshape(1)
    grads, place = together(grads, place)
    parts, beside = together(exchange(grads, NEAR), from_beside(ahead))
    shares = call(share_kernel, pieces, parts)
    shares, pair = together(shares, jnp.stack([ahead, beside]))
    parts, *others = together(
        exchange(shares, FAR), *(from_along(pair, steps) for steps in (1, 3, 2))
    )
    whole = exchange(call(share_kernel, pieces, parts), NEAR)
    fresh, shares = call(
        middle_kernel, (weights, pieces), whole, fast_init, place, pair, *others, flops=9 * 10**8,
        scratch=[pltpu.VMEM((DH, DH), BF16)] * 2,
    )
    y, squares = call(
        query_kernel,
        (shaped((2, 128, DH), F32), shaped((2, 128), F32)),
        queries, fast_init, fresh, out_gain.reshape(1, DH), flops=10**8,
    )
    squares = add_partner(add_partner(squares, 2), 4)
    parts, y, squares = together(exchange(shares, LOOP), y, squares)
    whole = exchange(call(share_kernel, pieces, parts), NEAR)
    final = call(last_kernel, weights, whole, fresh, flops=6 * 10**8)
    squares = add_partner(squares, 1)
    mixed = call(finish_kernel, shaped((2, 128, DH)), y, squares)
    return mixed, final


def solution(mesh):
    in_specs = (
        P(None, "tokens", "heads"),
        P(None, "tokens", "heads"),
        P(None, "tokens", "heads"),
        P(None, "heads", "tokens"),
        P("heads", None, None, None),
        P("heads"),
    )
    out_specs = (P(None, "tokens", "heads"), P("heads", None, None, None))
    return jax.shard_map(
        per_device, mesh=mesh, in_specs=in_specs, out_specs=out_specs, check_vma=False
    )
```

```python
import jax
import jax.numpy as jnp
from jax import lax
from jax.experimental import pallas as pl
from jax.experimental.pallas import tpu as pltpu
from jax.sharding import PartitionSpec as P

D = 2048
DH = 256
NS_STEPS = 2
PEERS = 8
SHARE = 3 * DH // PEERS
UNITS = DH // PEERS

coef_a = 3.4445
coef_b = -4.775
coef_c = 2.0315
step_size = 0.5

F32 = jnp.float32
BF16 = jnp.bfloat16


def token_index(x, y_hi, y_lo, z_hi):
    return ((x * 4 + y_hi) * 2 + y_lo) * 2 + z_hi


NEAR = [
    [token_index(x, y_hi, y_lo, z_hi) for x in range(4) for y_lo in range(2)]
    for y_hi in range(4)
    for z_hi in range(2)
]
FAR = [
    [token_index(x, y_hi, y_lo, z_hi) for y_hi in range(4) for z_hi in range(2)]
    for x in range(4)
    for y_lo in range(2)
]

def token_pairs(move):
    places = [(x, h, l, z) for x in range(4) for h in range(4) for l in range(2) for z in range(2)]
    return [(token_index(*p), token_index(*move(*p))) for p in places]


def from_beside(array):
    return lax.ppermute(array, "tokens", token_pairs(lambda x, h, l, z: (x, h, 1 - l, z)))


def from_along(array, steps):
    pairs = token_pairs(lambda x, h, l, z: ((x + steps) % 4, h, l, z))
    return lax.ppermute(array, "tokens", pairs)


def exchange(array, groups):
    return lax.all_to_all(array, "tokens", 0, 0, axis_index_groups=groups, tiled=True)


def mm(a, b, ca=1, cb=0):
    return lax.dot_general(a, b, (((ca,), (cb,)), ((), ())), preferred_element_type=F32)


def call(body, out_shape, *args, flops=0, scratch=(), space=pltpu.VMEM, limit=30):
    outs = out_shape if isinstance(out_shape, (tuple, list)) else [out_shape]
    moved = sum(a.size * a.dtype.itemsize for a in (*args, *outs))
    return pl.pallas_call(
        body,
        out_shape=out_shape,
        in_specs=[
            pl.BlockSpec(memory_space=pltpu.SMEM if a.dtype == jnp.int32 else space) for a in args
        ],
        out_specs=jax.tree.map(lambda _: pl.BlockSpec(memory_space=pltpu.VMEM), out_shape),
        scratch_shapes=list(scratch),
        compiler_params=pltpu.CompilerParams(vmem_limit_bytes=limit * 2**20),
        cost_estimate=pl.CostEstimate(flops=flops, bytes_accessed=moved, transcendentals=0),
    )(*args)


def scale_rows(rate_row, rows):
    tall = jnp.transpose(jnp.broadcast_to(rate_row, (128, rate_row.shape[1])))
    return (jnp.concatenate([tall, tall], axis=1) * rows.astype(F32)).astype(BF16)


def elementwise(gate, up, back):
    sig = jax.nn.sigmoid(gate)
    hidden = (gate * sig * up).astype(BF16)
    grad_gate = (back * up * sig * (1.0 + gate * (1.0 - sig))).astype(BF16)
    grad_up = (back * gate * sig).astype(BF16)
    return hidden, grad_gate, grad_up


def put_grads(out_ref, which, grad):
    grad = grad.astype(BF16)
    done = 0
    while done < DH:
        row = which * DH + done
        peer, inside = row // SHARE, row % SHARE
        count = min(SHARE - inside, DH - done)
        out_ref[peer, pl.ds(inside, count)] = grad[done : done + count]
        done += count


def local_grads(keys, scaled, gate_w, up_w, down_w, grads_ref):
    gate, up, back = mm(keys, gate_w), mm(keys, up_w), mm(scaled, down_w, 1, 1)
    hidden, grad_gate, grad_up = elementwise(gate, up, back)
    put_grads(grads_ref, 0, mm(keys, grad_gate, 0, 0))
    put_grads(grads_ref, 1, mm(keys, grad_up, 0, 0))
    put_grads(grads_ref, 2, mm(hidden, scaled, 0, 0))


def first_kernel(k_hbm, v_hbm, r_hbm, w_hbm, grads_ref, ahead_ref, k_ref, v_ref, r_ref, w_ref, sems):
    pairs = ((w_hbm, w_ref), (k_hbm, k_ref), (v_hbm, v_ref), (r_hbm, r_ref))
    copies = [pltpu.make_async_copy(a, b, sems.at[n]) for n, (a, b) in enumerate(pairs)]
    for copy in copies:
        copy.start()
    for copy in copies:
        copy.wait()
    scaled = scale_rows(r_ref[0], v_ref[0])
    local_grads(k_ref[0], scaled, w_ref[0, 0], w_ref[0, 1], w_ref[0, 2], grads_ref)
    ahead_ref[0] = k_ref[1]
    ahead_ref[1] = scale_rows(r_ref[1], v_ref[1])


def share_kernel(parts_ref, copies_ref):
    total = parts_ref[0].astype(F32)
    for peer in range(1, parts_ref.shape[0]):
        total = total + parts_ref[peer].astype(F32)
    total = total.astype(BF16)
    for peer in range(copies_ref.shape[0]):
        copies_ref[peer] = total


def newton_update(stacked, w_ref):
    current = []
    for m in range(3):
        wide = stacked[m].astype(F32)
        square = jnp.sum(jnp.sum(wide * wide, axis=0, keepdims=True), axis=1, keepdims=True)
        current.append((wide * (1.0 / (jnp.sqrt(square) + 1e-07))).astype(BF16))
    for step in range(NS_STEPS):
        grams = [mm(x, x, 1, 1).astype(BF16) for x in current]
        squares = [mm(a, a) for a in grams]
        mixers = [
            (coef_b * a.astype(F32) + coef_c * s).astype(BF16) for a, s in zip(grams, squares)
        ]
        products = [mm(b, x) for b, x in zip(mixers, current)]
        current = [(coef_a * x.astype(F32) + p).astype(BF16) for x, p in zip(current, products)]
    return [
        (w_ref[0, m].astype(F32) + step_size * current[m].astype(F32)).astype(BF16)
        for m in range(3)
    ]


def middle_kernel(grads_ref, w_ref, place_ref, *refs):
    tokens, (fresh_ref, out_ref, gate_ref, up_ref) = refs[:4], refs[4:]
    fresh = newton_update(grads_ref[...].reshape(3, DH, DH), w_ref)
    for m in range(3):
        fresh_ref[0, m] = fresh[m]
    gate_ref[...] = jnp.transpose(fresh[0])
    up_ref[...] = jnp.transpose(fresh[1])
    units = pl.ds(pl.multiple_of(place_ref[0] * UNITS, UNITS), UNITS)
    pair_w = jnp.concatenate([gate_ref[units], up_ref[units]], axis=0)
    down_w = fresh_ref[0, 2, units]
    pair_sum, down_sum = jnp.zeros((2 * UNITS, DH), F32), jnp.zeros((UNITS, DH), F32)
    for token_ref in tokens:
        keys = token_ref[:, 0].reshape(256, DH)
        scaled = token_ref[:, 1].reshape(256, DH)
        gate_up = mm(pair_w, keys, 1, 1)
        back = mm(down_w, scaled, 1, 1)
        hidden, grad_gate, grad_up = elementwise(gate_up[:UNITS], gate_up[UNITS:], back)
        pair_sum = pair_sum + mm(jnp.concatenate([grad_gate, grad_up], axis=0), keys)
        down_sum = down_sum + mm(hidden, scaled)
    sums = pair_sum[:UNITS], pair_sum[UNITS:], down_sum
    for m in range(3):
        part = sums[m].astype(BF16)
        for peer in range(PEERS):
            out_ref[peer, pl.ds(m * UNITS, UNITS)] = part


def last_kernel(grads_ref, w_ref, fresh_ref):
    rows = [grads_ref[:, m * UNITS : (m + 1) * UNITS].reshape(DH, DH) for m in range(3)]
    stacked = [jnp.transpose(rows[0]), jnp.transpose(rows[1]), rows[2]]
    fresh = newton_update(stacked, w_ref)
    for m in range(3):
        fresh_ref[0, m] = fresh[m]


def query_kernel(q_ref, w0_ref, w1_ref, gain_ref, y_ref, squares_ref):
    for block, w_ref in enumerate((w0_ref, w1_ref)):
        gate = mm(q_ref[block], w_ref[0, 0])
        up = mm(q_ref[block], w_ref[0, 1])
        hidden = (gate * jax.nn.sigmoid(gate) * up).astype(BF16)
        out = mm(hidden, w_ref[0, 2])
        y_ref[block] = out * gain_ref[...]
        sums = jnp.sum(out * out, axis=1, keepdims=True)
        squares_ref[pl.ds(block, 1)] = jnp.transpose(jnp.broadcast_to(sums, (128, 128)))[:1]


def finish_kernel(y_ref, squares_ref, out_ref):
    root = jnp.sqrt(squares_ref[...] / D + 1e-06)
    for block in range(2):
        tall = jnp.transpose(jnp.broadcast_to(root[block : block + 1], (128, 128)))
        both = jnp.concatenate([tall, tall], axis=1)
        out_ref[block] = (y_ref[block] / both).astype(BF16)


def shaped(shape, dtype=BF16):
    return jax.ShapeDtypeStruct(shape, dtype)


def add_partner(squares, bit):
    pairs = [(h, h ^ bit) for h in range(8)]
    return squares + lax.ppermute(squares, "heads", pairs)


def together(*values):
    return lax.optimization_barrier(values)


def per_device(queries, keys, values, rates, fast_init, out_gain):
    pieces = shaped((PEERS, SHARE, DH))
    weights = shaped((1, 3, DH, DH))
    copied = [(2, 128, DH), (2, 128, DH), (2, 1, 128), (1, 3, DH, DH)]
    own = [pltpu.VMEM(shape, F32 if shape[1] == 1 else BF16) for shape in copied]
    grads, ahead = call(
        first_kernel, (pieces, shaped((2, 128, DH))), keys, values, rates, fast_init, flops=10**8,
        scratch=[*own, pltpu.SemaphoreType.DMA((4,))], space=pl.ANY, limit=58,
    )
    token = lax.axis_index("tokens")
    place = (token // 16 * 2 + token // 2 % 2).reshape(1)
    grads, place = together(grads, place)
    parts, beside = together(exchange(grads, NEAR), from_beside(ahead))
    shares = call(share_kernel, pieces, parts)
    pair = jnp.stack([ahead, beside])
    parts, *others = together(
        exchange(shares, FAR), *(from_along(pair, steps) for steps in (1, 3, 2))
    )
    whole = exchange(call(share_kernel, pieces, parts), NEAR)
    fresh, shares = call(
        middle_kernel, (weights, pieces), whole, fast_init, place, pair, *others, flops=9 * 10**8,
        scratch=[pltpu.VMEM((DH, DH), BF16)] * 2,
    )
    y, squares = call(
        query_kernel,
        (shaped((2, 128, DH), F32), shaped((2, 128), F32)),
        queries, fast_init, fresh, out_gain.reshape(1, DH), flops=10**8,
    )
    squares = add_partner(add_partner(squares, 2), 4)
    parts, y, squares = together(exchange(shares, FAR), y, squares)
    whole = exchange(call(share_kernel, pieces, parts), NEAR)
    final = call(last_kernel, weights, whole, fresh, flops=6 * 10**8)
    squares = add_partner(squares, 1)
    mixed = call(finish_kernel, shaped((2, 128, DH)), y, squares)
    return mixed, final


def solution(mesh):
    in_specs = (
        P(None, "tokens", "heads"),
        P(None, "tokens", "heads"),
        P(None, "tokens", "heads"),
        P(None, "heads", "tokens"),
        P("heads", None, None, None),
        P("heads"),
    )
    out_specs = (P(None, "tokens", "heads"), P("heads", None, None, None))
    return jax.shard_map(
        per_device, mesh=mesh, in_specs=in_specs, out_specs=out_specs, check_vma=False
    )
```
